32 devices in a mesh: groups: 2 (over x), rows: 16 (over z, y, core).
Axes of the slice: x: 2, y: 2, z: 4, core: 2. Of those that a mesh axis runs over, the one named last changes fastest.
Arguments:
- frame_maps: bfloat16 [64, 2, 48, 64, 128], P(('groups', 'rows')), parts along dimension 0, may hold values from -6 to 6
- net_state: bfloat16 [128, 48, 64, 128], P(('groups', 'rows')), parts along dimension 0, may hold values from -3 to 3
- edges: int32 [128, 2], P('groups'), parts along dimension 0, may hold values from 0 to 31, as said below
- offsets: int32 [128, 2], P(('groups', 'rows')), parts along dimension 0, may hold values from -8 to 8
- w_motion: bfloat16 [81, 128], replicated, may hold values from -0.625 to 0.625
- w_input: bfloat16 [256, 384], replicated, may hold values from -0.375 to 0.375
- w_gates: bfloat16 [1152, 256], replicated, may hold values from -0.1875 to 0.1875
- w_candidate: bfloat16 [1152, 128], replicated, may hold values from -0.1875 to 0.1875
- w_aggregate: bfloat16 [1152, 128], replicated, may hold values from -0.1875 to 0.1875
Outputs:
- new_state: bfloat16 [128, 48, 64, 128], P(('groups', 'rows')), parts along dimension 0
- frame_update: bfloat16 [64, 48, 64, 128], P(('groups', 'rows')), parts along dimension 0
The draws below stay inside these ranges and needn't reach their ends.
There are 2 independent parts, one for each index of `groups`. The reference program is written for one: setup_inputs(seed, part) draws one part's arguments, and reference() takes and returns one part's arrays. A program takes and returns all parts, laid end to end along the dimension named above; an argument that names none is the same for every part. Nothing has to cross between parts.
Inputs may be any that keep to these rules, and one draw needn't show every extreme that they name: `edges`: edge e lies with the frames of index k = e // 4 of rows (frames k * 2 to (k + 1) * 2 - 1); its source and target are frames of indices k - 1, k or k + 1, and differ.
All inputs are finite; a program needn't handle non-finite values.
Results may differ from the reference program's by a relative error of at most 0.006.
Values may be sent and summed in bfloat16 or wider, within the bound.
No kernel may reach another device: no remote copies, remote signals or barrier semaphores. Data moves between devices by JAX's collectives and lax.ppermute only.
A program may use at most 128 MiB of HBM per device.

```python
import jax
import jax.numpy as jnp
from jax import lax

CH = 128
HT = 48
WD = 64
RADIUS = 4
SHIFT = 8
FR_DEV = 2
EDGE_DEV = 4
FRAMES = 32
EDGES = 64
DISP = 81


def draw_edges(key, part):
    device_count = FRAMES // FR_DEV
    edge_ids = jnp.arange(EDGES, dtype=jnp.int32)
    owner = edge_ids // EDGE_DEV
    slot = edge_ids % EDGE_DEV
    keys = jax.random.split(key, 4)
    source_dev = owner + jax.random.randint(keys[0], (EDGES,), -1, 2, dtype=jnp.int32)
    target_dev = owner + jax.random.randint(keys[1], (EDGES,), -1, 2, dtype=jnp.int32)
    source_dev = jnp.where(slot == 0, owner - 1, source_dev)
    target_dev = jnp.where(slot == 1, owner + 1, target_dev)
    source_dev = jnp.clip(source_dev, 0, device_count - 1)
    target_dev = jnp.clip(target_dev, 0, device_count - 1)
    source = source_dev * FR_DEV + jax.random.randint(keys[2], (EDGES,), 0, FR_DEV, dtype=jnp.int32)
    source = jnp.where((owner == 0) & (slot == 0), 0, source)
    source = jnp.where((owner == device_count - 1) & (slot == 1), FRAMES - 1, source)
    target = target_dev * FR_DEV + jax.random.randint(keys[3], (EDGES,), 0, FR_DEV, dtype=jnp.int32)
    upper = jnp.minimum((owner + 2) * FR_DEV, FRAMES) - 1
    target = jnp.where(target == source, jnp.where(source + 1 <= upper, source + 1, source - 1), target)
    return jnp.stack([source, target], axis=1).astype(jnp.int32)


def place_ends(values, stream_key, smallest, largest):
    shape = values.shape
    spot = [jax.random.randint(jax.random.fold_in(stream_key, axis), (), 0, shape[axis]) for axis in range(len(shape))]
    values = values.at[tuple(spot)].set(smallest)
    longest = shape.index(max(shape))
    spot[longest] = (spot[longest] + 1) % shape[longest]
    return values.at[tuple(spot)].set(largest)


def shard_levels(rng, dims, cuts, smallest, largest):
    factor_of = 1.0
    for dim, blocks in cuts:
        steps = jax.random.uniform(jax.random.fold_in(jax.random.fold_in(rng, 6), dim), (blocks,), jnp.float32, smallest / len(cuts), largest / len(cuts))
        factor_of = factor_of * jnp.repeat(jnp.exp(steps), dims[dim] // blocks).reshape((-1,) + (1,) * (len(dims) - 1 - dim))
    return factor_of


def gaussian(key, shape, deviation, limit, cuts=(), kind=jnp.bfloat16):
    loudness = shard_levels(key, shape, cuts, -0.22, 0.18) if cuts else 1.0
    array = jax.random.normal(key, shape, jnp.float32) * deviation * loudness
    return jnp.minimum(jnp.maximum(array, -limit), limit).astype(kind)


def setup_inputs(seed: int = 0, part: int = 0) -> dict:
    arg_keys = jax.random.split(jax.random.key(seed), 10)
    part_keys = jax.random.split(jax.random.fold_in(arg_keys[9], part), 10)
    return {
        "frame_maps": gaussian(part_keys[0], (FRAMES, 2, HT, WD, CH), 1.0, 6.0, ((0, 16),)),
        "net_state": gaussian(part_keys[1], (EDGES, HT, WD, CH), 0.5, 3.0, ((0, 16),)),
        "edges": draw_edges(jax.random.fold_in(jax.random.fold_in(arg_keys[9], part), 71), part),
        "offsets": place_ends(jax.random.randint(part_keys[3], (EDGES, 2), 0 - SHIFT, SHIFT + 1), jax.random.fold_in(part_keys[3], 1), 0 - SHIFT, SHIFT).astype(jnp.int32),
        "w_motion": gaussian(arg_keys[4], (DISP, CH), DISP ** -0.5, 0.625),
        "w_input": gaussian(arg_keys[5], (2 * CH, 3 * CH), (2 * CH) ** -0.5, 0.375),
        "w_gates": gaussian(arg_keys[6], (9 * CH, 2 * CH), (9 * CH) ** -0.5, 0.1875),
        "w_candidate": gaussian(arg_keys[7], (9 * CH, CH), (9 * CH) ** -0.5, 0.1875),
        "w_aggregate": gaussian(arg_keys[8], (9 * CH, CH), (9 * CH) ** -0.5, 0.1875),
    }


def conv_columns(field):
    height, width_px, chans = field.shape
    padded = jnp.pad(field, ((1, 1), (1, 1), (0, 0)))
    pieces = [padded[row_step:row_step + height, col_step:col_step + width_px, :] for row_step in range(3) for col_step in range(3)]
    return jnp.concatenate(pieces, axis=-1).reshape(height * width_px, 9 * chans)


def correlate(source_feat, target_feat, offset_pair):
    height, width_px, chans = source_feat.shape
    margin = SHIFT + RADIUS
    span = 2 * RADIUS + 1
    padded = jnp.pad(target_feat, ((margin, margin), (margin, margin), (0, 0)))
    start_row = (SHIFT + offset_pair[0]).astype(jnp.int32)
    start_col = (SHIFT + offset_pair[1]).astype(jnp.int32)
    window = lax.dynamic_slice(padded, (start_row, start_col, jnp.int32(0)), (height + span - 1, width_px + span - 1, chans))
    planes = []
    for row_step in range(span):
        for col_step in range(span):
            tile = window[row_step:row_step + height, col_step:col_step + width_px, :]
            planes.append(jnp.einsum("hwc,hwc->hw", source_feat.astype(jnp.float32), tile.astype(jnp.float32)))
    volume = jnp.stack(planes, axis=0)
    return (volume.reshape(span * span, height * width_px) * (chans ** -0.5)).astype(jnp.bfloat16)


def edge_update(source_feat, target_feat, context, state, offset_pair, w_motion, w_input, w_gates, w_candidate):
    height, width_px, chans = state.shape
    volume = correlate(source_feat, target_feat, offset_pair)
    motion = jax.nn.relu(jnp.einsum("kp,kc->pc", volume.astype(jnp.float32), w_motion.astype(jnp.float32))).astype(jnp.bfloat16)
    flat_ctx = context.reshape(height * width_px, chans)
    flat_state = state.reshape(height * width_px, chans).astype(jnp.float32)
    inputs = jnp.dot(motion, w_input[:chans], preferred_element_type=jnp.float32) + jnp.dot(flat_ctx, w_input[chans:], preferred_element_type=jnp.float32)
    gates = jnp.dot(conv_columns(state), w_gates, preferred_element_type=jnp.float32)
    update_gate = jax.nn.sigmoid(gates[:, :chans] + inputs[:, :chans])
    reset_gate = jax.nn.sigmoid(gates[:, chans:] + inputs[:, chans:2 * chans])
    reset_state = (reset_gate * flat_state).astype(jnp.bfloat16).reshape(height, width_px, chans)
    candidate = jnp.tanh(jnp.dot(conv_columns(reset_state), w_candidate, preferred_element_type=jnp.float32) + inputs[:, 2 * chans:])
    fresh = (1.0 - update_gate) * flat_state + update_gate * candidate
    return fresh.astype(jnp.bfloat16).reshape(height, width_px, chans)


def aggregate(mean_map, w_aggregate):
    height, width_px, chans = mean_map.shape
    return jnp.dot(conv_columns(mean_map), w_aggregate, preferred_element_type=jnp.float32).astype(jnp.bfloat16).reshape(height, width_px, chans)


def reference(frame_maps, net_state, edges, offsets, w_motion, w_input, w_gates, w_candidate, w_aggregate):
    def one_edge(item):
        pair, shift_pair, state = item
        source_pair = lax.dynamic_index_in_dim(frame_maps, pair[0], 0, keepdims=False)
        target_pair = lax.dynamic_index_in_dim(frame_maps, pair[1], 0, keepdims=False)
        return edge_update(source_pair[0], target_pair[0], source_pair[1], state, shift_pair, w_motion, w_input, w_gates, w_candidate)

    new_state = lax.map(one_edge, (edges, offsets, net_state))
    edge_ids = jnp.arange(EDGES, dtype=jnp.int32)
    owner = (edge_ids // EDGE_DEV).astype(jnp.int32)
    slot_ids = (owner * (3 * FR_DEV) + edges[:, 0] - (owner - 1) * FR_DEV).astype(jnp.int32)
    partial_sums = jax.ops.segment_sum(new_state.astype(jnp.float32), slot_ids, num_segments=3 * FRAMES)
    partial_sums = partial_sums.astype(jnp.bfloat16)
    all_slots = jnp.arange(3 * FRAMES, dtype=jnp.int32)
    slot_frame = ((all_slots // (3 * FR_DEV) - 1) * FR_DEV + all_slots % (3 * FR_DEV)).astype(jnp.int32)
    slot_frame = jnp.clip(slot_frame, 0, FRAMES - 1).astype(jnp.int32)
    sums = jnp.zeros((FRAMES,) + new_state.shape[1:], jnp.float32).at[slot_frame].add(partial_sums.astype(jnp.float32))
    counts = jnp.zeros((FRAMES,), jnp.float32).at[edges[:, 0]].add(jnp.ones((EDGES,), jnp.float32))
    mean_state = (sums / jnp.maximum(counts, 1.0)[:, None, None, None]).astype(jnp.bfloat16)

    def one_frame(mean_map):
        return aggregate(mean_map, w_aggregate)

    frame_update = lax.map(one_frame, mean_state)
    return (new_state, frame_update)
```

```python
import functools

import jax
import jax.numpy as jnp
from jax import lax
from jax.experimental import pallas as pl
from jax.experimental.pallas import tpu as pltpu
from jax.sharding import PartitionSpec as P

RADIUS = 4
SHIFT = 8
SPAN = 2 * RADIUS + 1
MARGIN = SHIFT + RADIUS
F32 = jnp.float32
BF16 = jnp.bfloat16
VMEM_LIMIT = 56 << 20


def any_spec():
    return pl.BlockSpec(memory_space=pl.ANY)


def whole(array):
    return pl.BlockSpec(array.shape, lambda *_: (0,) * array.ndim)


def fetch(cases, dst, sem):
    for condition, src in cases:

        @pl.when(condition)
        def _(src=src):
            pltpu.make_async_copy(src, dst, sem).start()


def await_copy(dst, sem):
    pltpu.make_async_copy(dst, dst, sem).wait()


def neighbours(block):
    rows, width, chans = block.shape
    flat = block.reshape(rows * width, chans)
    x = lax.broadcasted_iota(jnp.int32, (rows, width, chans), 1).reshape(rows * width, chans)
    left = jnp.where(x == 0, 0.0, pltpu.roll(flat, 1, 0)).astype(BF16)
    right = jnp.where(x == width - 1, 0.0, pltpu.roll(flat, rows * width - 1, 0)).astype(BF16)
    return [side.reshape(rows, width, chans) for side in (left, flat.astype(BF16), right)]


def put_columns(columns, start, block):
    chans = block.shape[-1]
    rows = block.shape[0]
    for i, side in enumerate(neighbours(block)):
        columns[pl.ds(start, rows), :, i * chans : (i + 1) * chans] = side


def conv_rows(columns, start, rows, weights):
    width, depth = columns.shape[1:]
    taps = [columns[pl.ds(start + step, rows)].reshape(rows * width, depth) for step in range(3)]
    return jnp.dot(jnp.concatenate(taps, axis=1), weights, preferred_element_type=F32)


def sigmoid(v):
    return 0.5 * jnp.tanh(0.5 * v) + 0.5


def gates_kernel(state_ref, weights_ref, out_ref, columns):
    height, width, chans = state_ref.shape[1:]
    edge_row = jnp.zeros((1,) + columns.shape[1:], BF16)
    columns[0:1] = edge_row
    columns[height + 1 :] = edge_row
    step = 8
    for y in range(0, height, step):
        put_columns(columns, y + 1, state_ref[0, y : y + step].astype(F32))
    weights = weights_ref[...]
    for y in range(0, height, step):
        gates = conv_rows(columns, y, step, weights)
        out_ref[0, y : y + step] = gates.astype(BF16).reshape(step, width, weights.shape[1])


def gates_of(state, weights):
    edges, height, width, chans = state.shape
    outs = weights.shape[1]
    return pl.pallas_call(
        gates_kernel,
        grid=(edges,),
        in_specs=[pl.BlockSpec((1, height, width, chans), lambda e: (e, 0, 0, 0)), whole(weights)],
        out_specs=pl.BlockSpec((1, height, width, outs), lambda e: (e, 0, 0, 0)),
        out_shape=jax.ShapeDtypeStruct((edges, height, width, outs), BF16),
        scratch_shapes=[pltpu.VMEM((height + 2, width, 3 * chans), BF16)],
        compiler_params=pltpu.CompilerParams(vmem_limit_bytes=VMEM_LIMIT),
        cost_estimate=pl.CostEstimate(
            flops=2 * edges * height * width * 9 * chans * outs,
            bytes_accessed=2 * edges * height * width * (chans + outs),
            transcendentals=0,
        ),
        name="gates",
    )(state, weights)


def motion_kernel(meta, own, near, far, flip_ref, mask_ref, base_ref, out_ref, src_buf, raw_buf, tgt_buf, w_buf, sems):
    edge = pl.program_id(0)
    edges = pl.num_programs(0)
    height, width, chans = own.shape[2:]
    slot = lax.rem(edge, 2)
    lanes = 2 * width
    tiles = base_ref.shape[0]

    def start(e, s):
        def cases(buf, frame):
            return ((buf == 0, own.at[frame, 0]), (buf == 1, far.at[frame]), (buf == 2, near.at[frame, 0]))

        fetch(cases(meta[e, 0], meta[e, 1]), src_buf.at[s, pl.ds(1, height)], sems.at[0, s])
        fetch(cases(meta[e, 2], meta[e, 3]), raw_buf.at[s], sems.at[1, s])

    @pl.when(edge == 0)
    def _():
        start(edge, slot)
        tgt_buf[0:MARGIN] = jnp.zeros((MARGIN, width, chans), BF16)
        below = tgt_buf.shape[0] - MARGIN - height
        tgt_buf[MARGIN + height :] = jnp.zeros((below, width, chans), BF16)

    @pl.when(edge + 1 < edges)
    def _():
        start(edge + 1, 1 - slot)

    oy, ox = meta[edge, 4], meta[edge, 5]
    for j in range(tiles):
        w_buf[j * lanes : (j + 1) * lanes] = pltpu.roll(base_ref[j], lax.rem(lanes - ox, lanes), 0).astype(BF16)

    await_copy(src_buf.at[slot, pl.ds(1, height)], sems.at[0, slot])
    await_copy(raw_buf.at[slot], sems.at[1, slot])

    flip = flip_ref[...]
    for y in range(0, height, 2):
        block = raw_buf[slot, y : y + 2].reshape(lanes, chans)
        turned = jnp.dot(flip, block, preferred_element_type=F32).astype(BF16)
        tgt_buf[MARGIN + y : MARGIN + y + 2] = turned.reshape(2, width, chans)

    mask = mask_ref[...]
    keep = mask != 0.0
    odd = lax.rem(oy + 2 * SHIFT, 2)
    weights = w_buf[...]
    unroll = 5

    @pl.loop(0, (height // 2 + unroll) // unroll)
    def _(i):
        starts = [2 * (i * unroll + u) - odd for u in range(unroll)]
        scores = []
        for y in starts:
            lhs = src_buf[slot, pl.ds(y + 1, 2)].reshape(lanes, chans)
            rhs = tgt_buf[pl.ds(y + oy - RADIUS + MARGIN, 2 * tiles)].reshape(tiles * lanes, chans)
            scores.append(lax.dot_general(lhs, rhs, (((1,), (1,)), ((), ())), preferred_element_type=F32))
        for y, pair in zip(starts, scores):
            volume = []
            for r in range(2):
                parts = []
                for j in range(tiles):
                    tile = pair[r * width : (r + 1) * width, j * lanes : (j + 1) * lanes] * (chans**-0.5)
                    tile = pltpu.roll(tile.astype(BF16), 0, 1, stride=1, stride_axis=0)
                    parts.append(jnp.where(keep, tile.astype(F32), 0.0).astype(BF16))
                volume.append(jnp.concatenate(parts, axis=1))
            res = jnp.dot(jnp.concatenate(volume, axis=0), weights, preferred_element_type=F32)
            out_ref[0, pl.ds(y + 1, 1)] = jnp.maximum(res[:width, :chans], 0.0).astype(BF16)[None]
            out_ref[0, pl.ds(y + 2, 1)] = jnp.maximum(res[width:, chans:], 0.0).astype(BF16)[None]


def motion_of(meta, own, near, far, w_motion):
    _, _, height, width, chans = own.shape
    edges = meta.shape[0]
    lanes = 2 * width
    rows = SPAN + 1
    taps = jnp.flip(w_motion.reshape(SPAN, SPAN, chans).astype(F32), axis=1)
    blank = jnp.zeros((1, SPAN, chans), F32)
    both = jnp.concatenate(
        [jnp.concatenate([taps, blank], axis=0), jnp.concatenate([blank, taps], axis=0)], axis=2
    )
    low = width - 1 - RADIUS
    padded = jnp.pad(both, ((0, 0), (0, lanes - SPAN), (0, 0))).reshape(rows // 2, 2, lanes, 2 * chans)
    base = jnp.roll(padded[:, 0], low, axis=1) + jnp.roll(padded[:, 1], low + width, axis=1)
    flip = jnp.kron(jnp.eye(2, dtype=F32), jnp.eye(width, dtype=F32)[::-1]).astype(BF16)
    x = jnp.arange(width)[:, None]
    lane = jnp.arange(lanes)[None]
    middle = (lane >= width // 2) & (lane < width + width // 2)
    inside = jnp.where(middle, (lane >= x) & (lane < x + width), jnp.where(lane < width, x > lane, lane >= x + width))
    mask = inside.astype(F32)
    buffer_rows = height + 4
    target_rows = height + 2 * MARGIN + 2
    return pl.pallas_call(
        motion_kernel,
        grid_spec=pltpu.PrefetchScalarGridSpec(
            num_scalar_prefetch=1,
            grid=(edges,),
            in_specs=[any_spec(), any_spec(), any_spec(), whole(flip), whole(mask), whole(base)],
            out_specs=pl.BlockSpec((1, buffer_rows, width, chans), lambda e, m: (e, 0, 0, 0)),
            scratch_shapes=[
                pltpu.VMEM((2, buffer_rows, width, chans), BF16),
                pltpu.VMEM((2, height, width, chans), BF16),
                pltpu.VMEM((target_rows, width, chans), BF16),
                pltpu.VMEM((rows * width, 2 * chans), BF16),
                pltpu.SemaphoreType.DMA((2, 2)),
            ],
        ),
        out_shape=jax.ShapeDtypeStruct((edges, buffer_rows, width, chans), BF16),
        compiler_params=pltpu.CompilerParams(vmem_limit_bytes=VMEM_LIMIT),
        cost_estimate=pl.CostEstimate(
            flops=8 * edges * height * width * chans * rows * width,
            bytes_accessed=6 * edges * height * width * chans,
            transcendentals=0,
        ),
        name="motion",
    )(meta, own, near, far, flip, mask, base)


def gru_kernel(
    first,
    last,
    split,
    meta,
    own,
    near,
    far_top,
    far_low,
    motion,
    gates,
    state,
    w_input,
    w_candidate,
    alias,
    new_ref,
    own_sum,
    near_sum,
    far_sum,
    ctx_buf,
    motion_buf,
    gates_buf,
    state_buf,
    columns,
    update_buf,
    drive_buf,
    totals,
    sems,
):
    edge = pl.program_id(0)
    edges = pl.num_programs(0)
    frames = own.shape[0]
    height, width, chans = own.shape[2:]
    slot = lax.rem(edge, 2)
    top = max(first - 1, 0)
    end = min(last + 1, height)
    rows = end - top

    def start(e, s):
        buf, frame = meta[e, 0], meta[e, 1]
        pltpu.make_async_copy(motion.at[e, pl.ds(top + 1, rows)], motion_buf.at[s], sems.at[1, s]).start()
        pltpu.make_async_copy(gates.at[e, pl.ds(top, rows)], gates_buf.at[s], sems.at[2, s]).start()
        pltpu.make_async_copy(state.at[e, pl.ds(top, rows)], state_buf.at[s], sems.at[3, s]).start()
        above = min(max(split - top, 0), rows)
        for piece, far, low, high, sem in ((0, far_top, 0, above, 0), (1, far_low, above, rows, 4)):
            if high > low:
                base = top + low
                fetch(
                    (
                        (buf == 0, own.at[frame, 1, pl.ds(base, high - low)]),
                        (buf == 1, far.at[frame, pl.ds(base - piece * split, high - low)]),
                        (buf == 2, near.at[frame, 1, pl.ds(base, high - low)]),
                    ),
                    ctx_buf.at[s, pl.ds(low, high - low)],
                    sems.at[sem, s],
                )

    def finish(s):
        await_copy(motion_buf.at[s], sems.at[1, s])
        await_copy(gates_buf.at[s], sems.at[2, s])
        await_copy(state_buf.at[s], sems.at[3, s])
        above = min(max(split - top, 0), rows)
        for low, high, sem in ((0, above, 0), (above, rows, 4)):
            if high > low:
                await_copy(ctx_buf.at[s, pl.ds(low, high - low)], sems.at[sem, s])

    @pl.when(edge == 0)
    def _():
        start(edge, slot)
        edge_row = jnp.zeros((1,) + columns.shape[1:], BF16)
        columns[0:1] = edge_row
        columns[rows + 1 :] = edge_row
        totals[...] = jnp.zeros(totals.shape, F32)

    @pl.when(edge + 1 < edges)
    def _():
        start(edge + 1, 1 - slot)

    finish(slot)

    weights = w_input[...]
    step = 5
    for y in range(0, rows, step):
        count = min(step, rows - y)
        span = slice(y, y + count)
        mixed = jnp.concatenate([motion_buf[slot, span], ctx_buf[slot, span]], axis=-1)
        inputs = jnp.dot(mixed.reshape(count * width, 2 * chans), weights, preferred_element_type=F32)
        inputs = inputs.reshape(count, width, 3 * chans)
        pre = gates_buf[slot, span].astype(F32)
        update_buf[span] = sigmoid(pre[..., :chans] + inputs[..., :chans])
        reset = sigmoid(pre[..., chans:] + inputs[..., chans : 2 * chans])
        drive_buf[span] = inputs[..., 2 * chans :]
        held = (reset * state_buf[slot, span].astype(F32)).astype(BF16).astype(F32)
        put_columns(columns, y + 1, held)

    weights = w_candidate[...]
    place = meta[edge, 0] * frames + meta[edge, 1]
    step = 8
    for y in range(first, last, step):
        count = min(step, last - y)
        span = slice(y - top, y - top + count)
        conv = conv_rows(columns, y - top, count, weights).reshape(count, width, chans)
        candidate = jnp.tanh(conv + drive_buf[span])
        update = update_buf[span]
        fresh = ((1.0 - update) * state_buf[slot, span].astype(F32) + update * candidate).astype(BF16)
        new_ref[0, y - first : y - first + count] = fresh
        totals[place, y - first : y - first + count] += fresh.astype(F32)

    @pl.when(edge == edges - 1)
    def _():
        for i, out in enumerate((own_sum, far_sum, near_sum)):
            out[...] = totals[i * frames : (i + 1) * frames].astype(BF16)


def gru_of(band, split, meta, own, near, far_top, far_low, motion, gates, state, w_input, w_candidate, earlier):
    frames, _, height, width, chans = own.shape
    edges = state.shape[0]
    size = height // 2
    first, last = band * size, (band + 1) * size
    rows = min(last + 1, height) - max(first - 1, 0)
    sums = jax.ShapeDtypeStruct((frames, size, width, chans), BF16)
    sum_spec = pl.BlockSpec(sums.shape, lambda e, m: (0, 0, 0, 0))
    body = functools.partial(gru_kernel, first, last, split)
    operands = [meta, own, near, far_top, far_low, motion, gates, state, w_input, w_candidate]
    if earlier is None:
        kernel = lambda *refs: body(*refs[:10], None, *refs[10:])
        aliases = {}
    else:
        kernel = body
        operands.append(earlier)
        aliases = {10: 0}
    return pl.pallas_call(
        kernel,
        grid_spec=pltpu.PrefetchScalarGridSpec(
            num_scalar_prefetch=1,
            grid=(edges,),
            in_specs=[any_spec()] * 7 + [whole(w_input), whole(w_candidate)] + [any_spec()] * (len(operands) - 10),
            out_specs=[pl.BlockSpec((1, size, width, chans), lambda e, m: (e, band, 0, 0)), sum_spec, sum_spec, sum_spec],
            scratch_shapes=[
                pltpu.VMEM((2, rows, width, chans), BF16),
                pltpu.VMEM((2, rows, width, chans), BF16),
                pltpu.VMEM((2, rows, width, 2 * chans), BF16),
                pltpu.VMEM((2, rows, width, chans), BF16),
                pltpu.VMEM((rows + 2, width, 3 * chans), BF16),
                pltpu.VMEM((rows, width, chans), F32),
                pltpu.VMEM((rows, width, chans), F32),
                pltpu.VMEM((3 * frames, size, width, chans), F32),
                pltpu.SemaphoreType.DMA((5, 2)),
            ],
        ),
        out_shape=[jax.ShapeDtypeStruct(state.shape, BF16), sums, sums, sums],
        input_output_aliases=aliases,
        compiler_params=pltpu.CompilerParams(vmem_limit_bytes=VMEM_LIMIT),
        cost_estimate=pl.CostEstimate(
            flops=2 * edges * rows * width * chans * (6 * chans + 9 * chans),
            bytes_accessed=2 * edges * rows * width * chans * 6,
            transcendentals=3 * edges * rows * width * chans,
        ),
        name=f"gru_band{band}",
    )(*operands)


def aggregate_kernel(counts, *refs):
    sums, weights_ref, out_ref, columns = refs[:-3], refs[-3], refs[-2], refs[-1]
    bands = [sums[i : i + 3] for i in range(0, len(sums), 3)]
    frame = pl.program_id(0)
    height, width, chans = out_ref.shape[1:]
    size = height // len(bands)
    edge_row = jnp.zeros((1,) + columns.shape[1:], BF16)
    columns[0:1] = edge_row
    columns[height + 1 :] = edge_row
    count = counts[frame]
    step = 8
    for band, (a, b, c) in enumerate(bands):
        for y in range(0, size, step):
            span = slice(y, y + step)
            total = a[0, span].astype(F32) + b[0, span].astype(F32) + c[0, span].astype(F32)
            mean = (total / count).astype(BF16).astype(F32)
            put_columns(columns, band * size + y + 1, mean)
    weights = weights_ref[...]
    for y in range(0, height, step):
        out = conv_rows(columns, y, step, weights)
        out_ref[0, y : y + step] = out.astype(BF16).reshape(step, width, chans)


def aggregate_of(counts, bands, weights):
    frames, size, width, chans = bands[0][0].shape
    height = size * len(bands)
    sums = [array for band in bands for array in band]
    return pl.pallas_call(
        aggregate_kernel,
        grid_spec=pltpu.PrefetchScalarGridSpec(
            num_scalar_prefetch=1,
            grid=(frames,),
            in_specs=[pl.BlockSpec((1, size, width, chans), lambda f, c: (f, 0, 0, 0))] * len(sums) + [whole(weights)],
            out_specs=pl.BlockSpec((1, height, width, chans), lambda f, c: (f, 0, 0, 0)),
            scratch_shapes=[pltpu.VMEM((height + 2, width, 3 * chans), BF16)],
        ),
        out_shape=jax.ShapeDtypeStruct((frames, height, width, chans), BF16),
        compiler_params=pltpu.CompilerParams(vmem_limit_bytes=VMEM_LIMIT),
        name="aggregate",
    )(counts, *sums, weights)


def per_device(
    frame_maps, net_state, edges, offsets, w_motion, w_input, w_gates, w_candidate, w_aggregate
):
    frames, _, height, width, chans = frame_maps.shape
    edge_count = net_state.shape[0]
    me = lax.axis_index("rows")
    count = lax.axis_size("rows")
    near_route = [(i, i ^ 1) for i in range(count)]
    far_route = [(i, i + 1 if i % 2 else i - 1) for i in range(1, count - 1)]

    def far_swap(block):
        return lax.ppermute(block, "rows", far_route)

    def near_swap(block):
        return lax.ppermute(block, "rows", near_route)

    split = height // 2 + 1
    far_feat = far_swap(frame_maps[:, 0])
    near = near_swap(frame_maps)
    far_top = far_swap(frame_maps[:, 1, :split])
    far_low = far_swap(frame_maps[:, 1, split:])

    my_edges = lax.dynamic_slice_in_dim(edges, me * edge_count, edge_count, 0)
    owner = my_edges // frames
    buf = jnp.where(owner == me, 0, jnp.where(owner == (me ^ 1), 2, 1))
    local = my_edges % frames
    meta = jnp.stack(
        [buf[:, 0], local[:, 0], buf[:, 1], local[:, 1], offsets[:, 0], offsets[:, 1]], axis=1
    ).astype(jnp.int32)
    mine = me * frames + jnp.arange(frames, dtype=jnp.int32)
    counts = jnp.maximum(jnp.sum((edges[:, 0][:, None] == mine[None]).astype(F32), axis=0), 1.0)

    gates = gates_of(net_state, w_gates)
    motion = motion_of(meta, frame_maps, near, far_feat, w_motion)
    new_state = None
    bands = []
    for band in range(2):
        new_state, own_sum, near_sum, far_sum = gru_of(
            band, split, meta, frame_maps, near, far_top, far_low if band else far_top,
            motion, gates, net_state, w_input, w_candidate, new_state,
        )
        bands.append((own_sum, near_swap(near_sum), far_swap(far_sum)))
    frame_update = aggregate_of(counts, bands, w_aggregate)
    return (new_state, frame_update)


def solution(mesh):
    in_specs = (
        P(("groups", "rows"), None, None, None, None),
        P(("groups", "rows"), None, None, None),
        P("groups", None),
        P(("groups", "rows"), None),
        P(),
        P(),
        P(),
        P(),
        P(),
    )
    out_specs = (P(("groups", "rows"), None, None, None), P(("groups", "rows"), None, None, None))
    return jax.shard_map(
        per_device, mesh=mesh, in_specs=in_specs, out_specs=out_specs, check_vma=False
    )
```

```python
import functools

import jax
import jax.numpy as jnp
from jax import lax
from jax.experimental import pallas as pl
from jax.experimental.pallas import tpu as pltpu
from jax.sharding import PartitionSpec as P

RADIUS = 4
SHIFT = 8
SPAN = 2 * RADIUS + 1
MARGIN = SHIFT + RADIUS
F32 = jnp.float32
BF16 = jnp.bfloat16
VMEM_LIMIT = 60 << 20


def any_spec():
    return pl.BlockSpec(memory_space=pl.ANY)


def whole(array):
    return pl.BlockSpec(array.shape, lambda *_: (0,) * array.ndim)


def fetch(cases, dst, sem):
    for condition, src in cases:

        @pl.when(condition)
        def _(src=src):
            pltpu.make_async_copy(src, dst, sem).start()


def await_copy(dst, sem):
    pltpu.make_async_copy(dst, dst, sem).wait()


def neighbours(block):
    rows, width, chans = block.shape
    flat = block.reshape(rows * width, chans)
    x = lax.broadcasted_iota(jnp.int32, (rows, width, chans), 1).reshape(rows * width, chans)
    left = jnp.where(x == 0, 0.0, pltpu.roll(flat, 1, 0)).astype(BF16)
    right = jnp.where(x == width - 1, 0.0, pltpu.roll(flat, rows * width - 1, 0)).astype(BF16)
    return [side.reshape(rows, width, chans) for side in (left, flat.astype(BF16), right)]


def put_columns(columns, start, block):
    chans = block.shape[-1]
    rows = block.shape[0]
    for i, side in enumerate(neighbours(block)):
        columns[pl.ds(start, rows), :, i * chans : (i + 1) * chans] = side


def conv_rows(columns, start, rows, weights):
    width, depth = columns.shape[1:]
    taps = [columns[pl.ds(start + step, rows)].reshape(rows * width, depth) for step in range(3)]
    return jnp.dot(jnp.concatenate(taps, axis=1), weights, preferred_element_type=F32)


def sigmoid(v):
    return 0.5 * jnp.tanh(0.5 * v) + 0.5


def gates_kernel(state_ref, weights_ref, out_ref, columns):
    height, width, chans = state_ref.shape[1:]
    edge_row = jnp.zeros((1,) + columns.shape[1:], BF16)
    columns[0:1] = edge_row
    columns[height + 1 :] = edge_row
    step = 8
    for y in range(0, height, step):
        put_columns(columns, y + 1, state_ref[0, y : y + step].astype(F32))
    weights = weights_ref[...]
    for y in range(0, height, step):
        gates = conv_rows(columns, y, step, weights)
        out_ref[0, y : y + step] = gates.astype(BF16).reshape(step, width, weights.shape[1])


def gates_of(state, weights):
    edges, height, width, chans = state.shape
    outs = weights.shape[1]
    return pl.pallas_call(
        gates_kernel,
        grid=(edges,),
        in_specs=[pl.BlockSpec((1, height, width, chans), lambda e: (e, 0, 0, 0)), whole(weights)],
        out_specs=pl.BlockSpec((1, height, width, outs), lambda e: (e, 0, 0, 0)),
        out_shape=jax.ShapeDtypeStruct((edges, height, width, outs), BF16),
        scratch_shapes=[pltpu.VMEM((height + 2, width, 3 * chans), BF16)],
        compiler_params=pltpu.CompilerParams(vmem_limit_bytes=VMEM_LIMIT),
        cost_estimate=pl.CostEstimate(
            flops=2 * edges * height * width * 9 * chans * outs,
            bytes_accessed=2 * edges * height * width * (chans + outs),
            transcendentals=0,
        ),
        name="gates",
    )(state, weights)


def motion_kernel(meta, own, near, far, flip_ref, mask_ref, base_ref, out_ref, src_buf, raw_buf, tgt_buf, w_buf, sems):
    edge = pl.program_id(0)
    edges = pl.num_programs(0)
    height, width, chans = own.shape[2:]
    slot = lax.rem(edge, 2)
    lanes = 2 * width
    tiles = base_ref.shape[0]

    def start(e, s):
        def cases(buf, frame):
            return ((buf == 0, own.at[frame, 0]), (buf == 1, far.at[frame]), (buf == 2, near.at[frame, 0]))

        fetch(cases(meta[e, 0], meta[e, 1]), src_buf.at[s, pl.ds(1, height)], sems.at[0, s])
        fetch(cases(meta[e, 2], meta[e, 3]), raw_buf.at[s], sems.at[1, s])

    @pl.when(edge == 0)
    def _():
        start(edge, slot)
        tgt_buf[0:MARGIN] = jnp.zeros((MARGIN, width, chans), BF16)
        below = tgt_buf.shape[0] - MARGIN - height
        tgt_buf[MARGIN + height :] = jnp.zeros((below, width, chans), BF16)

    @pl.when(edge + 1 < edges)
    def _():
        start(edge + 1, 1 - slot)

    oy, ox = meta[edge, 4], meta[edge, 5]
    for j in range(tiles):
        w_buf[j * lanes : (j + 1) * lanes] = pltpu.roll(base_ref[j], lax.rem(lanes - ox, lanes), 0).astype(BF16)

    await_copy(src_buf.at[slot, pl.ds(1, height)], sems.at[0, slot])
    await_copy(raw_buf.at[slot], sems.at[1, slot])

    flip = flip_ref[...]
    for y in range(0, height, 2):
        block = raw_buf[slot, y : y + 2].reshape(lanes, chans)
        turned = jnp.dot(flip, block, preferred_element_type=F32).astype(BF16)
        tgt_buf[MARGIN + y : MARGIN + y + 2] = turned.reshape(2, width, chans)

    mask = mask_ref[...]
    keep = mask != 0.0
    odd = lax.rem(oy + 2 * SHIFT, 2)
    weights = w_buf[...]
    unroll = 5

    @pl.loop(0, (height // 2 + unroll) // unroll)
    def _(i):
        starts = [2 * (i * unroll + u) - odd for u in range(unroll)]
        scores = []
        for y in starts:
            lhs = src_buf[slot, pl.ds(y + 1, 2)].reshape(lanes, chans)
            rhs = tgt_buf[pl.ds(y + oy - RADIUS + MARGIN, 2 * tiles)].reshape(tiles * lanes, chans)
            scores.append(lax.dot_general(lhs, rhs, (((1,), (1,)), ((), ())), preferred_element_type=F32))
        for y, pair in zip(starts, scores):
            volume = []
            for r in range(2):
                parts = []
                for j in range(tiles):
                    tile = pair[r * width : (r + 1) * width, j * lanes : (j + 1) * lanes] * (chans**-0.5)
                    tile = pltpu.roll(tile.astype(BF16), 0, 1, stride=1, stride_axis=0)
                    parts.append(jnp.where(keep, tile.astype(F32), 0.0).astype(BF16))
                volume.append(jnp.concatenate(parts, axis=1))
            res = jnp.dot(jnp.concatenate(volume, axis=0), weights, preferred_element_type=F32)
            out_ref[0, pl.ds(y + 1, 1)] = jnp.maximum(res[:width, :chans], 0.0).astype(BF16)[None]
            out_ref[0, pl.ds(y + 2, 1)] = jnp.maximum(res[width:, chans:], 0.0).astype(BF16)[None]


def motion_of(meta, own, near, far, w_motion):
    _, _, height, width, chans = own.shape
    edges = meta.shape[0]
    lanes = 2 * width
    rows = SPAN + 1
    taps = jnp.flip(w_motion.reshape(SPAN, SPAN, chans).astype(F32), axis=1)
    blank = jnp.zeros((1, SPAN, chans), F32)
    both = jnp.concatenate(
        [jnp.concatenate([taps, blank], axis=0), jnp.concatenate([blank, taps], axis=0)], axis=2
    )
    low = width - 1 - RADIUS
    padded = jnp.pad(both, ((0, 0), (0, lanes - SPAN), (0, 0))).reshape(rows // 2, 2, lanes, 2 * chans)
    base = jnp.roll(padded[:, 0], low, axis=1) + jnp.roll(padded[:, 1], low + width, axis=1)
    flip = jnp.kron(jnp.eye(2, dtype=F32), jnp.eye(width, dtype=F32)[::-1]).astype(BF16)
    x = jnp.arange(width)[:, None]
    lane = jnp.arange(lanes)[None]
    middle = (lane >= width // 2) & (lane < width + width // 2)
    inside = jnp.where(middle, (lane >= x) & (lane < x + width), jnp.where(lane < width, x > lane, lane >= x + width))
    mask = inside.astype(F32)
    buffer_rows = height + 4
    target_rows = height + 2 * MARGIN + 2
    return pl.pallas_call(
        motion_kernel,
        grid_spec=pltpu.PrefetchScalarGridSpec(
            num_scalar_prefetch=1,
            grid=(edges,),
            in_specs=[any_spec(), any_spec(), any_spec(), whole(flip), whole(mask), whole(base)],
            out_specs=pl.BlockSpec((1, buffer_rows, width, chans), lambda e, m: (e, 0, 0, 0)),
            scratch_shapes=[
                pltpu.VMEM((2, buffer_rows, width, chans), BF16),
                pltpu.VMEM((2, height, width, chans), BF16),
                pltpu.VMEM((target_rows, width, chans), BF16),
                pltpu.VMEM((rows * width, 2 * chans), BF16),
                pltpu.SemaphoreType.DMA((2, 2)),
            ],
        ),
        out_shape=jax.ShapeDtypeStruct((edges, buffer_rows, width, chans), BF16),
        compiler_params=pltpu.CompilerParams(vmem_limit_bytes=VMEM_LIMIT),
        cost_estimate=pl.CostEstimate(
            flops=8 * edges * height * width * chans * rows * width,
            bytes_accessed=6 * edges * height * width * chans,
            transcendentals=0,
        ),
        name="motion",
    )(meta, own, near, far, flip, mask, base)


def gru_kernel(
    first,
    last,
    split,
    meta,
    own,
    near,
    far_top,
    far_low,
    motion,
    gates,
    state,
    w_input,
    w_candidate,
    alias,
    new_ref,
    own_sum,
    near_sum,
    far_sum,
    ctx_buf,
    motion_buf,
    gates_buf,
    state_buf,
    columns,
    update_buf,
    drive_buf,
    totals,
    sems,
):
    edge = pl.program_id(0)
    edges = pl.num_programs(0)
    frames = own.shape[0]
    height, width, chans = own.shape[2:]
    slot = lax.rem(edge, 2)
    top = max(first - 1, 0)
    end = min(last + 1, height)
    rows = end - top

    def start(e, s):
        buf, frame = meta[e, 0], meta[e, 1]
        pltpu.make_async_copy(motion.at[e, pl.ds(top + 1, rows)], motion_buf.at[s], sems.at[1, s]).start()
        pltpu.make_async_copy(gates.at[e, pl.ds(top, rows)], gates_buf.at[s], sems.at[2, s]).start()
        pltpu.make_async_copy(state.at[e, pl.ds(top, rows)], state_buf.at[s], sems.at[3, s]).start()
        above = min(max(split - top, 0), rows)
        for piece, far, low, high, sem in ((0, far_top, 0, above, 0), (1, far_low, above, rows, 4)):
            if high > low:
                base = top + low
                fetch(
                    (
                        (buf == 0, own.at[frame, 1, pl.ds(base, high - low)]),
                        (buf == 1, far.at[frame, pl.ds(base - piece * split, high - low)]),
                        (buf == 2, near.at[frame, 1, pl.ds(base, high - low)]),
                    ),
                    ctx_buf.at[s, pl.ds(low, high - low)],
                    sems.at[sem, s],
                )

    def finish(s):
        await_copy(motion_buf.at[s], sems.at[1, s])
        await_copy(gates_buf.at[s], sems.at[2, s])
        await_copy(state_buf.at[s], sems.at[3, s])
        above = min(max(split - top, 0), rows)
        for low, high, sem in ((0, above, 0), (above, rows, 4)):
            if high > low:
                await_copy(ctx_buf.at[s, pl.ds(low, high - low)], sems.at[sem, s])

    @pl.when(edge == 0)
    def _():
        start(edge, slot)
        edge_row = jnp.zeros((1,) + columns.shape[1:], BF16)
        columns[0:1] = edge_row
        columns[rows + 1 :] = edge_row
        totals[...] = jnp.zeros(totals.shape, F32)

    @pl.when(edge + 1 < edges)
    def _():
        start(edge + 1, 1 - slot)

    finish(slot)

    weights = w_input[...]
    step = 5
    for y in range(0, rows, step):
        count = min(step, rows - y)
        span = slice(y, y + count)
        mixed = jnp.concatenate([motion_buf[slot, span], ctx_buf[slot, span]], axis=-1)
        inputs = jnp.dot(mixed.reshape(count * width, 2 * chans), weights, preferred_element_type=F32)
        inputs = inputs.reshape(count, width, 3 * chans)
        pre = gates_buf[slot, span].astype(F32)
        update_buf[span] = sigmoid(pre[..., :chans] + inputs[..., :chans])
        reset = sigmoid(pre[..., chans:] + inputs[..., chans : 2 * chans])
        drive_buf[span] = inputs[..., 2 * chans :]
        held = (reset * state_buf[slot, span].astype(F32)).astype(BF16).astype(F32)
        put_columns(columns, y + 1, held)

    weights = w_candidate[...]
    place = meta[edge, 0] * frames + meta[edge, 1]
    step = 8
    for y in range(first, last, step):
        count = min(step, last - y)
        span = slice(y - top, y - top + count)
        conv = conv_rows(columns, y - top, count, weights).reshape(count, width, chans)
        candidate = jnp.tanh(conv + drive_buf[span])
        update = update_buf[span]
        fresh = ((1.0 - update) * state_buf[slot, span].astype(F32) + update * candidate).astype(BF16)
        new_ref[0, y - first : y - first + count] = fresh
        totals[place, y - first : y - first + count] += fresh.astype(F32)

    @pl.when(edge == edges - 1)
    def _():
        for i, out in enumerate((own_sum, far_sum, near_sum)):
            out[...] = totals[i * frames : (i + 1) * frames].astype(BF16)


def gru_of(band, split, meta, own, near, far_top, far_low, motion, gates, state, w_input, w_candidate, earlier):
    frames, _, height, width, chans = own.shape
    edges = state.shape[0]
    size = height // 2
    first, last = band * size, (band + 1) * size
    rows = min(last + 1, height) - max(first - 1, 0)
    sums = jax.ShapeDtypeStruct((frames, size, width, chans), BF16)
    sum_spec = pl.BlockSpec(sums.shape, lambda e, m: (0, 0, 0, 0))
    body = functools.partial(gru_kernel, first, last, split)
    operands = [meta, own, near, far_top, far_low, motion, gates, state, w_input, w_candidate]
    if earlier is None:
        kernel = lambda *refs: body(*refs[:10], None, *refs[10:])
        aliases = {}
    else:
        kernel = body
        operands.append(earlier)
        aliases = {10: 0}
    return pl.pallas_call(
        kernel,
        grid_spec=pltpu.PrefetchScalarGridSpec(
            num_scalar_prefetch=1,
            grid=(edges,),
            in_specs=[any_spec()] * 7 + [whole(w_input), whole(w_candidate)] + [any_spec()] * (len(operands) - 10),
            out_specs=[pl.BlockSpec((1, size, width, chans), lambda e, m: (e, band, 0, 0)), sum_spec, sum_spec, sum_spec],
            scratch_shapes=[
                pltpu.VMEM((2, rows, width, chans), BF16),
                pltpu.VMEM((2, rows, width, chans), BF16),
                pltpu.VMEM((2, rows, width, 2 * chans), BF16),
                pltpu.VMEM((2, rows, width, chans), BF16),
                pltpu.VMEM((rows + 2, width, 3 * chans), BF16),
                pltpu.VMEM((rows, width, chans), F32),
                pltpu.VMEM((rows, width, chans), F32),
                pltpu.VMEM((3 * frames, size, width, chans), F32),
                pltpu.SemaphoreType.DMA((5, 2)),
            ],
        ),
        out_shape=[jax.ShapeDtypeStruct(state.shape, BF16), sums, sums, sums],
        input_output_aliases=aliases,
        compiler_params=pltpu.CompilerParams(vmem_limit_bytes=VMEM_LIMIT),
        cost_estimate=pl.CostEstimate(
            flops=2 * edges * rows * width * chans * (6 * chans + 9 * chans),
            bytes_accessed=2 * edges * rows * width * chans * 6,
            transcendentals=3 * edges * rows * width * chans,
        ),
        name=f"gru_band{band}",
    )(*operands)


def aggregate_kernel(counts, *refs):
    sums, weights_ref, out_ref, columns = refs[:-3], refs[-3], refs[-2], refs[-1]
    bands = [sums[i : i + 3] for i in range(0, len(sums), 3)]
    frame = pl.program_id(0)
    height, width, chans = out_ref.shape[1:]
    size = height // len(bands)
    edge_row = jnp.zeros((1,) + columns.shape[1:], BF16)
    columns[0:1] = edge_row
    columns[height + 1 :] = edge_row
    count = counts[frame]
    step = 8
    for band, (a, b, c) in enumerate(bands):
        for y in range(0, size, step):
            span = slice(y, y + step)
            total = a[0, span].astype(F32) + b[0, span].astype(F32) + c[0, span].astype(F32)
            mean = (total / count).astype(BF16).astype(F32)
            put_columns(columns, band * size + y + 1, mean)
    weights = weights_ref[...]
    for y in range(0, height, step):
        out = conv_rows(columns, y, step, weights)
        out_ref[0, y : y + step] = out.astype(BF16).reshape(step, width, chans)


def aggregate_of(counts, bands, weights):
    frames, size, width, chans = bands[0][0].shape
    height = size * len(bands)
    sums = [array for band in bands for array in band]
    return pl.pallas_call(
        aggregate_kernel,
        grid_spec=pltpu.PrefetchScalarGridSpec(
            num_scalar_prefetch=1,
            grid=(frames,),
            in_specs=[pl.BlockSpec((1, size, width, chans), lambda f, c: (f, 0, 0, 0))] * len(sums) + [whole(weights)],
            out_specs=pl.BlockSpec((1, height, width, chans), lambda f, c: (f, 0, 0, 0)),
            scratch_shapes=[pltpu.VMEM((height + 2, width, 3 * chans), BF16)],
        ),
        out_shape=jax.ShapeDtypeStruct((frames, height, width, chans), BF16),
        compiler_params=pltpu.CompilerParams(vmem_limit_bytes=VMEM_LIMIT),
        name="aggregate",
    )(counts, *sums, weights)


def per_device(
    frame_maps, net_state, edges, offsets, w_motion, w_input, w_gates, w_candidate, w_aggregate
):
    frames, _, height, width, chans = frame_maps.shape
    edge_count = net_state.shape[0]
    me = lax.axis_index("rows")
    count = lax.axis_size("rows")
    near_route = [(i, i ^ 1) for i in range(count)]
    far_route = [(i, i + 1 if i % 2 else i - 1) for i in range(1, count - 1)]

    def far_swap(block, *after):
        if after:
            block = lax.optimization_barrier((block,) + after)[0]
        return lax.ppermute(block, "rows", far_route)

    def near_swap(block):
        return lax.ppermute(block, "rows", near_route)

    split = height // 2 + 1
    far_feat = far_swap(frame_maps[:, 0])
    near = near_swap(frame_maps)

    my_edges = lax.dynamic_slice_in_dim(edges, me * edge_count, edge_count, 0)
    owner = my_edges // frames
    buf = jnp.where(owner == me, 0, jnp.where(owner == (me ^ 1), 2, 1))
    local = my_edges % frames
    meta = jnp.stack(
        [buf[:, 0], local[:, 0], buf[:, 1], local[:, 1], offsets[:, 0], offsets[:, 1]], axis=1
    ).astype(jnp.int32)
    mine = me * frames + jnp.arange(frames, dtype=jnp.int32)
    counts = jnp.maximum(jnp.sum((edges[:, 0][:, None] == mine[None]).astype(F32), axis=0), 1.0)

    gates = gates_of(net_state, w_gates)
    far_top = far_swap(frame_maps[:, 1, :split], far_feat, gates)
    motion = motion_of(meta, frame_maps, near, far_feat, w_motion)
    far_low = far_swap(frame_maps[:, 1, split:], far_top, motion)
    new_state = None
    bands = []
    latest = far_low
    for band in range(2):
        new_state, own_sum, near_sum, far_sum = gru_of(
            band, split, meta, frame_maps, near, far_top, far_low if band else far_top,
            motion, gates, net_state, w_input, w_candidate, new_state,
        )
        latest = far_swap(far_sum, latest)
        bands.append((own_sum, near_swap(near_sum), latest))
    frame_update = aggregate_of(counts, bands, w_aggregate)
    return (new_state, frame_update)


def solution(mesh):
    in_specs = (
        P(("groups", "rows"), None, None, None, None),
        P(("groups", "rows"), None, None, None),
        P("groups", None),
        P(("groups", "rows"), None),
        P(),
        P(),
        P(),
        P(),
        P(),
    )
    out_specs = (P(("groups", "rows"), None, None, None), P(("groups", "rows"), None, None, None))
    return jax.shard_map(
        per_device, mesh=mesh, in_specs=in_specs, out_specs=out_specs, check_vma=False
    )
```

```python
import functools

import jax
import jax.numpy as jnp
import numpy as np
from jax import lax
from jax.experimental import pallas as pl
from jax.experimental.pallas import tpu as pltpu
from jax.sharding import PartitionSpec as P

RADIUS = 4
SHIFT = 8
SPAN = 2 * RADIUS + 1
MARGIN = SHIFT + RADIUS
F32 = jnp.float32
BF16 = jnp.bfloat16
VMEM_LIMIT = 60 << 20


def any_spec():
    return pl.BlockSpec(memory_space=pl.ANY)


def whole(array):
    return pl.BlockSpec(array.shape, lambda *_: (0,) * array.ndim)


def fetch(cases, dst, sem):
    for condition, src in cases:

        @pl.when(condition)
        def _(src=src):
            pltpu.make_async_copy(src, dst, sem).start()


def await_copy(dst, sem):
    pltpu.make_async_copy(dst, dst, sem).wait()


def neighbours(block):
    rows, width, chans = block.shape
    flat = block.reshape(rows * width, chans)
    x = lax.broadcasted_iota(jnp.int32, (rows, width, chans), 1).reshape(rows * width, chans)
    left = jnp.where(x == 0, 0.0, pltpu.roll(flat, 1, 0)).astype(BF16)
    right = jnp.where(x == width - 1, 0.0, pltpu.roll(flat, rows * width - 1, 0)).astype(BF16)
    return [side.reshape(rows, width, chans) for side in (left, flat.astype(BF16), right)]


def put_columns(columns, start, block):
    chans = block.shape[-1]
    rows = block.shape[0]
    for i, side in enumerate(neighbours(block)):
        columns[pl.ds(start, rows), :, i * chans : (i + 1) * chans] = side


def conv_rows(columns, start, rows, weights):
    width, depth = columns.shape[1:]
    taps = [columns[pl.ds(start + step, rows)].reshape(rows * width, depth) for step in range(3)]
    return jnp.dot(jnp.concatenate(taps, axis=1), weights, preferred_element_type=F32)


def sigmoid(v):
    return 0.5 * jnp.tanh(0.5 * v) + 0.5


def gates_kernel(state_ref, weights_ref, out_ref, columns):
    height, width, chans = state_ref.shape[1:]
    edge_row = jnp.zeros((1,) + columns.shape[1:], BF16)
    columns[0:1] = edge_row
    columns[height + 1 :] = edge_row
    step = 8
    for y in range(0, height, step):
        put_columns(columns, y + 1, state_ref[0, y : y + step].astype(F32))
    weights = weights_ref[...]
    for y in range(0, height, step):
        gates = conv_rows(columns, y, step, weights)
        out_ref[0, y : y + step] = gates.astype(BF16).reshape(step, width, weights.shape[1])


def gates_of(state, weights):
    edges, height, width, chans = state.shape
    outs = weights.shape[1]
    return pl.pallas_call(
        gates_kernel,
        grid=(edges,),
        in_specs=[pl.BlockSpec((1, height, width, chans), lambda e: (e, 0, 0, 0)), whole(weights)],
        out_specs=pl.BlockSpec((1, height, width, outs), lambda e: (e, 0, 0, 0)),
        out_shape=jax.ShapeDtypeStruct((edges, height, width, outs), BF16),
        scratch_shapes=[pltpu.VMEM((height + 2, width, 3 * chans), BF16)],
        compiler_params=pltpu.CompilerParams(vmem_limit_bytes=VMEM_LIMIT),
        cost_estimate=pl.CostEstimate(
            flops=2 * edges * height * width * 9 * chans * outs,
            bytes_accessed=2 * edges * height * width * (chans + outs),
            transcendentals=0,
        ),
        name="gates",
    )(state, weights)


def motion_kernel(low, meta, own, near, far, flip_ref, mask_ref, base_ref, out_ref, src_buf, raw_buf, tgt_buf, w_buf, sems):
    step = pl.program_id(0)
    steps = pl.num_programs(0)
    edge = step + low
    height, width, chans = own.shape[2:]
    slot = lax.rem(step, 2)
    lanes = 2 * width
    tiles = base_ref.shape[0]

    def start(e, s):
        def cases(buf, frame):
            return ((buf == 0, own.at[frame, 0]), (buf == 1, far.at[frame]), (buf == 2, near.at[frame, 0]))

        fetch(cases(meta[e, 0], meta[e, 1]), src_buf.at[s, pl.ds(1, height)], sems.at[0, s])
        fetch(cases(meta[e, 2], meta[e, 3]), raw_buf.at[s], sems.at[1, s])

    @pl.when(step == 0)
    def _():
        start(edge, slot)
        tgt_buf[0:MARGIN] = jnp.zeros((MARGIN, width, chans), BF16)
        below = tgt_buf.shape[0] - MARGIN - height
        tgt_buf[MARGIN + height :] = jnp.zeros((below, width, chans), BF16)

    @pl.when(step + 1 < steps)
    def _():
        start(edge + 1, 1 - slot)

    oy, ox = meta[edge, 4], meta[edge, 5]
    for j in range(tiles):
        w_buf[j * lanes : (j + 1) * lanes] = pltpu.roll(base_ref[j], lax.rem(lanes - ox, lanes), 0).astype(BF16)

    await_copy(src_buf.at[slot, pl.ds(1, height)], sems.at[0, slot])
    await_copy(raw_buf.at[slot], sems.at[1, slot])

    flip = flip_ref[...]
    for y in range(0, height, 2):
        block = raw_buf[slot, y : y + 2].reshape(lanes, chans)
        turned = jnp.dot(flip, block, preferred_element_type=F32).astype(BF16)
        tgt_buf[MARGIN + y : MARGIN + y + 2] = turned.reshape(2, width, chans)

    mask = mask_ref[...]
    keep = mask != 0.0
    odd = lax.rem(oy + 2 * SHIFT, 2)
    weights = w_buf[...]
    unroll = 5

    @pl.loop(0, (height // 2 + unroll) // unroll)
    def _(i):
        starts = [2 * (i * unroll + u) - odd for u in range(unroll)]
        scores = []
        for y in starts:
            lhs = src_buf[slot, pl.ds(y + 1, 2)].reshape(lanes, chans)
            rhs = tgt_buf[pl.ds(y + oy - RADIUS + MARGIN, 2 * tiles)].reshape(tiles * lanes, chans)
            scores.append(lax.dot_general(lhs, rhs, (((1,), (1,)), ((), ())), preferred_element_type=F32))
        for y, pair in zip(starts, scores):
            volume = []
            for r in range(2):
                parts = []
                for j in range(tiles):
                    tile = pair[r * width : (r + 1) * width, j * lanes : (j + 1) * lanes] * (chans**-0.5)
                    tile = pltpu.roll(tile.astype(BF16), 0, 1, stride=1, stride_axis=0)
                    parts.append(jnp.where(keep, tile.astype(F32), 0.0).astype(BF16))
                volume.append(jnp.concatenate(parts, axis=1))
            res = jnp.dot(jnp.concatenate(volume, axis=0), weights, preferred_element_type=F32)
            out_ref[0, pl.ds(y + 1, 1)] = jnp.maximum(res[:width, :chans], 0.0).astype(BF16)[None]
            out_ref[0, pl.ds(y + 2, 1)] = jnp.maximum(res[width:, chans:], 0.0).astype(BF16)[None]


def motion_constants(width, chans):
    lanes = 2 * width
    rows = SPAN + 1
    place = np.zeros((2, rows // 2, lanes, SPAN * SPAN), np.float32)
    for r in range(rows):
        for b in range(SPAN):
            lane = (width - 1 + RADIUS - b + width * (r % 2)) % lanes
            for parity in range(2):
                if 0 <= r - parity < SPAN:
                    place[parity, r // 2, lane, (r - parity) * SPAN + b] = 1.0
    flip = np.kron(np.eye(2), np.eye(width)[::-1])
    x = np.arange(width)[:, None]
    lane = np.arange(lanes)[None]
    middle = (lane >= width // 2) & (lane < width + width // 2)
    inside = np.where(middle, (lane >= x) & (lane < x + width), np.where(lane < width, x > lane, lane >= x + width))
    return place.astype(BF16), flip.astype(BF16), inside.astype(np.float32)


def motion_weights(w_motion, width):
    place = motion_constants(width, w_motion.shape[1])[0]
    return jnp.concatenate(
        [jnp.einsum("tlk,kc->tlc", side, w_motion, preferred_element_type=F32) for side in place], axis=2
    )


def motion_of(low, high, meta, own, near, far, base, earlier):
    _, _, height, width, chans = own.shape
    edges = meta.shape[0]
    rows = SPAN + 1
    _, flip, mask = motion_constants(width, chans)
    buffer_rows = height + 4
    target_rows = height + 2 * MARGIN + 2
    operands = [meta, own, near, far, flip, mask, base]
    body = functools.partial(motion_kernel, low)
    if earlier is None:
        kernel, aliases = body, {}
    else:
        kernel, aliases = lambda *refs: body(*refs[:7], *refs[8:]), {7: 0}
        operands.append(earlier)
    return pl.pallas_call(
        kernel,
        grid_spec=pltpu.PrefetchScalarGridSpec(
            num_scalar_prefetch=1,
            grid=(high - low,),
            in_specs=[any_spec()] * 3 + [whole(flip), whole(mask), whole(base)] + [any_spec()] * (len(operands) - 7),
            out_specs=pl.BlockSpec((1, buffer_rows, width, chans), lambda e, m: (e + low, 0, 0, 0)),
            scratch_shapes=[
                pltpu.VMEM((2, buffer_rows, width, chans), BF16),
                pltpu.VMEM((2, height, width, chans), BF16),
                pltpu.VMEM((target_rows, width, chans), BF16),
                pltpu.VMEM((rows * width, 2 * chans), BF16),
                pltpu.SemaphoreType.DMA((2, 2)),
            ],
        ),
        out_shape=jax.ShapeDtypeStruct((edges, buffer_rows, width, chans), BF16),
        input_output_aliases=aliases,
        compiler_params=pltpu.CompilerParams(vmem_limit_bytes=VMEM_LIMIT),
        cost_estimate=pl.CostEstimate(
            flops=8 * (high - low) * height * width * chans * rows * width,
            bytes_accessed=6 * (high - low) * height * width * chans,
            transcendentals=0,
        ),
        name=f"motion_from{low}",
    )(*operands)


def gru_kernel(
    first,
    last,
    split,
    meta,
    own,
    near,
    far_top,
    far_low,
    motion,
    gates,
    state,
    w_input,
    w_candidate,
    alias,
    new_ref,
    own_sum,
    near_sum,
    far_sum,
    ctx_buf,
    motion_buf,
    gates_buf,
    state_buf,
    columns,
    update_buf,
    drive_buf,
    totals,
    sems,
):
    edge = pl.program_id(0)
    edges = pl.num_programs(0)
    frames = own.shape[0]
    height, width, chans = own.shape[2:]
    slot = lax.rem(edge, 2)
    top = max(first - 1, 0)
    end = min(last + 1, height)
    rows = end - top

    def start(e, s):
        buf, frame = meta[e, 0], meta[e, 1]
        pltpu.make_async_copy(motion.at[e, pl.ds(top + 1, rows)], motion_buf.at[s], sems.at[1, s]).start()
        pltpu.make_async_copy(gates.at[e, pl.ds(top, rows)], gates_buf.at[s], sems.at[2, s]).start()
        pltpu.make_async_copy(state.at[e, pl.ds(top, rows)], state_buf.at[s], sems.at[3, s]).start()
        above = min(max(split - top, 0), rows)
        for piece, far, low, high, sem in ((0, far_top, 0, above, 0), (1, far_low, above, rows, 4)):
            if high > low:
                base = top + low
                fetch(
                    (
                        (buf == 0, own.at[frame, 1, pl.ds(base, high - low)]),
                        (buf == 1, far.at[frame, pl.ds(base - piece * split, high - low)]),
                        (buf == 2, near.at[frame, 1, pl.ds(base, high - low)]),
                    ),
                    ctx_buf.at[s, pl.ds(low, high - low)],
                    sems.at[sem, s],
                )

    def finish(s):
        await_copy(motion_buf.at[s], sems.at[1, s])
        await_copy(gates_buf.at[s], sems.at[2, s])
        await_copy(state_buf.at[s], sems.at[3, s])
        above = min(max(split - top, 0), rows)
        for low, high, sem in ((0, above, 0), (above, rows, 4)):
            if high > low:
                await_copy(ctx_buf.at[s, pl.ds(low, high - low)], sems.at[sem, s])

    @pl.when(edge == 0)
    def _():
        start(edge, slot)
        edge_row = jnp.zeros((1,) + columns.shape[1:], BF16)
        columns[0:1] = edge_row
        columns[rows + 1 :] = edge_row
        totals[...] = jnp.zeros(totals.shape, F32)

    @pl.when(edge + 1 < edges)
    def _():
        start(edge + 1, 1 - slot)

    finish(slot)

    weights = w_input[...]
    step = 5
    for y in range(0, rows, step):
        count = min(step, rows - y)
        span = slice(y, y + count)
        mixed = jnp.concatenate([motion_buf[slot, span], ctx_buf[slot, span]], axis=-1)
        inputs = jnp.dot(mixed.reshape(count * width, 2 * chans), weights, preferred_element_type=F32)
        inputs = inputs.reshape(count, width, 3 * chans)
        pre = gates_buf[slot, span].astype(F32)
        update_buf[span] = sigmoid(pre[..., :chans] + inputs[..., :chans])
        reset = sigmoid(pre[..., chans:] + inputs[..., chans : 2 * chans])
        drive_buf[span] = inputs[..., 2 * chans :]
        held = (reset * state_buf[slot, span].astype(F32)).astype(BF16).astype(F32)
        put_columns(columns, y + 1, held)

    weights = w_candidate[...]
    place = meta[edge, 0] * frames + meta[edge, 1]
    step = 8
    for y in range(first, last, step):
        count = min(step, last - y)
        span = slice(y - top, y - top + count)
        conv = conv_rows(columns, y - top, count, weights).reshape(count, width, chans)
        candidate = jnp.tanh(conv + drive_buf[span])
        update = update_buf[span]
        fresh = ((1.0 - update) * state_buf[slot, span].astype(F32) + update * candidate).astype(BF16)
        new_ref[0, y - first : y - first + count] = fresh
        totals[place, y - first : y - first + count] += fresh.astype(F32)

    @pl.when(edge == edges - 1)
    def _():
        for i, out in enumerate((own_sum, far_sum, near_sum)):
            out[...] = totals[i * frames : (i + 1) * frames].astype(BF16)


def gru_of(band, split, meta, own, near, far_top, far_low, motion, gates, state, w_input, w_candidate, earlier):
    frames, _, height, width, chans = own.shape
    edges = state.shape[0]
    size = height // 2
    first, last = band * size, (band + 1) * size
    rows = min(last + 1, height) - max(first - 1, 0)
    sums = jax.ShapeDtypeStruct((frames, size, width, chans), BF16)
    sum_spec = pl.BlockSpec(sums.shape, lambda e, m: (0, 0, 0, 0))
    body = functools.partial(gru_kernel, first, last, split)
    operands = [meta, own, near, far_top, far_low, motion, gates, state, w_input, w_candidate]
    if earlier is None:
        kernel = lambda *refs: body(*refs[:10], None, *refs[10:])
        aliases = {}
    else:
        kernel = body
        operands.append(earlier)
        aliases = {10: 0}
    return pl.pallas_call(
        kernel,
        grid_spec=pltpu.PrefetchScalarGridSpec(
            num_scalar_prefetch=1,
            grid=(edges,),
            in_specs=[any_spec()] * 7 + [whole(w_input), whole(w_candidate)] + [any_spec()] * (len(operands) - 10),
            out_specs=[pl.BlockSpec((1, size, width, chans), lambda e, m: (e, band, 0, 0)), sum_spec, sum_spec, sum_spec],
            scratch_shapes=[
                pltpu.VMEM((2, rows, width, chans), BF16),
                pltpu.VMEM((2, rows, width, chans), BF16),
                pltpu.VMEM((2, rows, width, 2 * chans), BF16),
                pltpu.VMEM((2, rows, width, chans), BF16),
                pltpu.VMEM((rows + 2, width, 3 * chans), BF16),
                pltpu.VMEM((rows, width, chans), F32),
                pltpu.VMEM((rows, width, chans), F32),
                pltpu.VMEM((3 * frames, size, width, chans), F32),
                pltpu.SemaphoreType.DMA((5, 2)),
            ],
        ),
        out_shape=[jax.ShapeDtypeStruct(state.shape, BF16), sums, sums, sums],
        input_output_aliases=aliases,
        compiler_params=pltpu.CompilerParams(vmem_limit_bytes=VMEM_LIMIT),
        cost_estimate=pl.CostEstimate(
            flops=2 * edges * rows * width * chans * (6 * chans + 9 * chans),
            bytes_accessed=2 * edges * rows * width * chans * 6,
            transcendentals=3 * edges * rows * width * chans,
        ),
        name=f"gru_band{band}",
    )(*operands)


def aggregate_kernel(pieces, first, last, counts, *refs):
    sums, weights_ref, rest = refs[: 3 * len(pieces)], refs[3 * len(pieces)], refs[3 * len(pieces) + 1 :]
    out_ref, columns = rest[-2:]
    width, chans = out_ref.shape[2:]
    edge_row = jnp.zeros((1,) + columns.shape[1:], BF16)
    columns[0:1] = edge_row
    columns[columns.shape[0] - 1 :] = edge_row
    count = counts[pl.program_id(0)]
    step = 8
    at = 1
    for i, (low, high) in enumerate(pieces):
        for y in range(low, high, step):
            span = slice(y, min(y + step, high))
            a, b, c = (ref[0, span].astype(F32) for ref in sums[3 * i : 3 * i + 3])
            mean = ((a + b + c) / count).astype(BF16).astype(F32)
            put_columns(columns, at, mean)
            at += mean.shape[0]
    base = 0
    if len(rest) == 3:
        out_ref[0, :first] = rest[0][0]
        base = first
    weights = weights_ref[...]
    skip = 0 if first == 0 else 1
    for y in range(0, last - first, step):
        rows = min(step, last - first - y)
        out = conv_rows(columns, y + skip, rows, weights)
        out_ref[0, base + y : base + y + rows] = out.astype(BF16).reshape(rows, width, chans)


def aggregate_of(first, last, pieces, bands, counts, weights, earlier):
    frames, size, width, chans = bands[0][0].shape
    sums = [array for band in bands for array in band]
    depth = sum(high - low for low, high in pieces)
    rows = last if earlier is not None else last - first
    operands = [counts, *sums, weights]
    more = []
    if earlier is not None:
        operands.append(earlier)
        more = [pl.BlockSpec((1,) + earlier.shape[1:], lambda f, c: (f, 0, 0, 0))]
    return pl.pallas_call(
        functools.partial(aggregate_kernel, pieces, first, last),
        grid_spec=pltpu.PrefetchScalarGridSpec(
            num_scalar_prefetch=1,
            grid=(frames,),
            in_specs=[pl.BlockSpec((1, size, width, chans), lambda f, c: (f, 0, 0, 0))] * len(sums)
            + [whole(weights)]
            + more,
            out_specs=pl.BlockSpec((1, rows, width, chans), lambda f, c: (f, 0, 0, 0)),
            scratch_shapes=[pltpu.VMEM((depth + 2, width, 3 * chans), BF16)],
        ),
        out_shape=jax.ShapeDtypeStruct((frames, rows, width, chans), BF16),
        compiler_params=pltpu.CompilerParams(vmem_limit_bytes=16 << 20),
        cost_estimate=pl.CostEstimate(
            flops=2 * frames * (last - first) * width * 9 * chans * chans,
            bytes_accessed=8 * frames * depth * width * chans,
            transcendentals=0,
        ),
        name=f"aggregate_from{first}",
    )(*operands)


def per_device(
    frame_maps, net_state, edges, offsets, w_motion, w_input, w_gates, w_candidate, w_aggregate
):
    frames, _, height, width, chans = frame_maps.shape
    edge_count = net_state.shape[0]
    me = lax.axis_index("rows")
    count = lax.axis_size("rows")
    near_route = [(i, i ^ 1) for i in range(count)]
    far_route = [(i, i + 1 if i % 2 else i - 1) for i in range(1, count - 1)]

    def far_swap(block, *after):
        if after:
            block = lax.optimization_barrier((block,) + after)[0]
        return lax.ppermute(block, "rows", far_route)

    def near_swap(block):
        return lax.ppermute(block, "rows", near_route)

    split = height // 2 + 1
    far_feat = far_swap(frame_maps[:, 0])
    near = near_swap(frame_maps)

    my_edges = lax.dynamic_slice_in_dim(edges, me * edge_count, edge_count, 0)
    owner = my_edges // frames
    buf = jnp.where(owner == me, 0, jnp.where(owner == (me ^ 1), 2, 1))
    local = my_edges % frames
    meta = jnp.stack(
        [buf[:, 0], local[:, 0], buf[:, 1], local[:, 1], offsets[:, 0], offsets[:, 1]], axis=1
    ).astype(jnp.int32)
    mine = me * frames + jnp.arange(frames, dtype=jnp.int32)
    counts = jnp.maximum(jnp.sum((edges[:, 0][:, None] == mine[None]).astype(F32), axis=0), 1.0)

    base = motion_weights(w_motion, width)
    gates = gates_of(net_state, lax.optimization_barrier((w_gates, near))[0])
    half = edge_count // 2
    held_meta = lax.optimization_barrier((meta, gates))[0]
    motion = motion_of(0, half, held_meta, frame_maps, near, far_feat, base, None)
    far_top = far_swap(frame_maps[:, 1, :split], motion)
    motion = motion_of(half, edge_count, meta, frame_maps, near, far_feat, base, motion)
    far_low = far_swap(frame_maps[:, 1, split:], far_top, motion)
    size = height // 2

    def gru(band, earlier):
        return gru_of(
            band, split, meta, frame_maps, near, far_top, far_low if band else far_top,
            motion, gates, net_state, w_input, w_candidate, earlier,
        )

    new_state, own_sum, near_sum, far_sum = gru(0, None)
    far_first = far_swap(far_sum, far_low)
    near_first = near_swap(near_sum)
    first_sums = (own_sum, near_first, far_first)
    new_state, own_sum, near_sum, far_sum = gru(1, new_state)
    far_second = far_swap(far_sum, far_first)
    near_second = near_swap(near_sum)
    second_sums = (own_sum, near_second, far_second)
    upper = aggregate_of(0, size - 1, ((0, size),), (first_sums,), counts, w_aggregate, None)
    frame_update = aggregate_of(
        size - 1, height, ((size - 2, size), (0, size)), (first_sums, second_sums), counts, w_aggregate, upper
    )
    return (new_state, frame_update)


def solution(mesh):
    in_specs = (
        P(("groups", "rows"), None, None, None, None),
        P(("groups", "rows"), None, None, None),
        P("groups", None),
        P(("groups", "rows"), None),
        P(),
        P(),
        P(),
        P(),
        P(),
    )
    out_specs = (P(("groups", "rows"), None, None, None), P(("groups", "rows"), None, None, None))
    return jax.shard_map(
        per_device, mesh=mesh, in_specs=in_specs, out_specs=out_specs, check_vma=False
    )
```

```python
import functools

import jax
import jax.numpy as jnp
import numpy as np
from jax import lax
from jax.experimental import pallas as pl
from jax.experimental.pallas import tpu as pltpu
from jax.sharding import PartitionSpec as P

RADIUS = 4
SHIFT = 8
SPAN = 2 * RADIUS + 1
MARGIN = SHIFT + RADIUS
F32 = jnp.float32
BF16 = jnp.bfloat16
VMEM_LIMIT = 60 << 20


def any_spec():
    return pl.BlockSpec(memory_space=pl.ANY)


def whole(array):
    return pl.BlockSpec(array.shape, lambda *_: (0,) * array.ndim)


def fetch(cases, dst, sem):
    for condition, src in cases:

        @pl.when(condition)
        def _(src=src):
            pltpu.make_async_copy(src, dst, sem).start()


def await_copy(dst, sem):
    pltpu.make_async_copy(dst, dst, sem).wait()


def neighbours(block):
    rows, width, chans = block.shape
    flat = block.reshape(rows * width, chans)
    x = lax.broadcasted_iota(jnp.int32, (rows, width, chans), 1).reshape(rows * width, chans)
    left = jnp.where(x == 0, 0.0, pltpu.roll(flat, 1, 0)).astype(BF16)
    right = jnp.where(x == width - 1, 0.0, pltpu.roll(flat, rows * width - 1, 0)).astype(BF16)
    return [side.reshape(rows, width, chans) for side in (left, flat.astype(BF16), right)]


def put_columns(columns, start, block):
    chans = block.shape[-1]
    rows = block.shape[0]
    for i, side in enumerate(neighbours(block)):
        columns[pl.ds(start, rows), :, i * chans : (i + 1) * chans] = side


def conv_rows(columns, start, rows, weights):
    width, depth = columns.shape[1:]
    taps = [columns[pl.ds(start + step, rows)].reshape(rows * width, depth) for step in range(3)]
    return jnp.dot(jnp.concatenate(taps, axis=1), weights, preferred_element_type=F32)


def sigmoid(v):
    return 0.5 * jnp.tanh(0.5 * v) + 0.5


def gates_kernel(state_ref, weights_ref, out_ref, columns):
    height, width, chans = state_ref.shape[1:]
    edge_row = jnp.zeros((1,) + columns.shape[1:], BF16)
    columns[0:1] = edge_row
    columns[height + 1 :] = edge_row
    step = 8
    for y in range(0, height, step):
        put_columns(columns, y + 1, state_ref[0, y : y + step].astype(F32))
    weights = weights_ref[...]
    for y in range(0, height, step):
        gates = conv_rows(columns, y, step, weights)
        out_ref[0, y : y + step] = gates.astype(BF16).reshape(step, width, weights.shape[1])


def gates_of(state, weights):
    edges, height, width, chans = state.shape
    outs = weights.shape[1]
    return pl.pallas_call(
        gates_kernel,
        grid=(edges,),
        in_specs=[pl.BlockSpec((1, height, width, chans), lambda e: (e, 0, 0, 0)), whole(weights)],
        out_specs=pl.BlockSpec((1, height, width, outs), lambda e: (e, 0, 0, 0)),
        out_shape=jax.ShapeDtypeStruct((edges, height, width, outs), BF16),
        scratch_shapes=[pltpu.VMEM((height + 2, width, 3 * chans), BF16)],
        compiler_params=pltpu.CompilerParams(vmem_limit_bytes=VMEM_LIMIT),
        cost_estimate=pl.CostEstimate(
            flops=2 * edges * height * width * 9 * chans * outs,
            bytes_accessed=2 * edges * height * width * (chans + outs),
            transcendentals=0,
        ),
        name="gates",
    )(state, weights)


def motion_kernel(low, meta, own, near, far, flip_ref, mask_ref, base_ref, out_ref, src_buf, raw_buf, tgt_buf, w_buf, sems):
    step = pl.program_id(0)
    steps = pl.num_programs(0)
    edge = step + low
    height, width, chans = own.shape[2:]
    slot = lax.rem(step, 2)
    lanes = 2 * width
    tiles = base_ref.shape[0]

    def start(e, s):
        def cases(buf, frame):
            return ((buf == 0, own.at[frame, 0]), (buf == 1, far.at[frame]), (buf == 2, near.at[frame, 0]))

        fetch(cases(meta[e, 0], meta[e, 1]), src_buf.at[s, pl.ds(1, height)], sems.at[0, s])
        fetch(cases(meta[e, 2], meta[e, 3]), raw_buf.at[s], sems.at[1, s])

    @pl.when(step == 0)
    def _():
        start(edge, slot)
        tgt_buf[0:MARGIN] = jnp.zeros((MARGIN, width, chans), BF16)
        below = tgt_buf.shape[0] - MARGIN - height
        tgt_buf[MARGIN + height :] = jnp.zeros((below, width, chans), BF16)

    @pl.when(step + 1 < steps)
    def _():
        start(edge + 1, 1 - slot)

    oy, ox = meta[edge, 4], meta[edge, 5]
    for j in range(tiles):
        w_buf[j * lanes : (j + 1) * lanes] = pltpu.roll(base_ref[j], lax.rem(lanes - ox, lanes), 0).astype(BF16)

    await_copy(src_buf.at[slot, pl.ds(1, height)], sems.at[0, slot])
    await_copy(raw_buf.at[slot], sems.at[1, slot])

    flip = flip_ref[...]
    for y in range(0, height, 2):
        block = raw_buf[slot, y : y + 2].reshape(lanes, chans)
        turned = jnp.dot(flip, block, preferred_element_type=F32).astype(BF16)
        tgt_buf[MARGIN + y : MARGIN + y + 2] = turned.reshape(2, width, chans)

    mask = mask_ref[...]
    keep = mask != 0.0
    odd = lax.rem(oy + 2 * SHIFT, 2)
    weights = w_buf[...]
    unroll = 5

    @pl.loop(0, (height // 2 + unroll) // unroll)
    def _(i):
        starts = [2 * (i * unroll + u) - odd for u in range(unroll)]
        scores = []
        for y in starts:
            lhs = src_buf[slot, pl.ds(y + 1, 2)].reshape(lanes, chans)
            rhs = tgt_buf[pl.ds(y + oy - RADIUS + MARGIN, 2 * tiles)].reshape(tiles * lanes, chans)
            scores.append(lax.dot_general(lhs, rhs, (((1,), (1,)), ((), ())), preferred_element_type=F32))
        for y, pair in zip(starts, scores):
            volume = []
            for r in range(2):
                parts = []
                for j in range(tiles):
                    tile = pair[r * width : (r + 1) * width, j * lanes : (j + 1) * lanes] * (chans**-0.5)
                    tile = pltpu.roll(tile.astype(BF16), 0, 1, stride=1, stride_axis=0)
                    parts.append(jnp.where(keep, tile.astype(F32), 0.0).astype(BF16))
                volume.append(jnp.concatenate(parts, axis=1))
            res = jnp.dot(jnp.concatenate(volume, axis=0), weights, preferred_element_type=F32)
            out_ref[0, pl.ds(y + 1, 1)] = jnp.maximum(res[:width, :chans], 0.0).astype(BF16)[None]
            out_ref[0, pl.ds(y + 2, 1)] = jnp.maximum(res[width:, chans:], 0.0).astype(BF16)[None]


def motion_constants(width, chans):
    lanes = 2 * width
    rows = SPAN + 1
    place = np.zeros((2, rows // 2, lanes, SPAN * SPAN), np.float32)
    for r in range(rows):
        for b in range(SPAN):
            lane = (width - 1 + RADIUS - b + width * (r % 2)) % lanes
            for parity in range(2):
                if 0 <= r - parity < SPAN:
                    place[parity, r // 2, lane, (r - parity) * SPAN + b] = 1.0
    flip = np.kron(np.eye(2), np.eye(width)[::-1])
    x = np.arange(width)[:, None]
    lane = np.arange(lanes)[None]
    middle = (lane >= width // 2) & (lane < width + width // 2)
    inside = np.where(middle, (lane >= x) & (lane < x + width), np.where(lane < width, x > lane, lane >= x + width))
    return place.astype(BF16), flip.astype(BF16), inside.astype(np.float32)


def motion_weights(w_motion, width):
    place = motion_constants(width, w_motion.shape[1])[0]
    return jnp.concatenate(
        [jnp.einsum("tlk,kc->tlc", side, w_motion, preferred_element_type=F32) for side in place], axis=2
    )


def motion_of(low, high, meta, own, near, far, base, earlier):
    _, _, height, width, chans = own.shape
    edges = meta.shape[0]
    rows = SPAN + 1
    _, flip, mask = motion_constants(width, chans)
    buffer_rows = height + 4
    target_rows = height + 2 * MARGIN + 2
    operands = [meta, own, near, far, flip, mask, base]
    body = functools.partial(motion_kernel, low)
    if earlier is None:
        kernel, aliases = body, {}
    else:
        kernel, aliases = lambda *refs: body(*refs[:7], *refs[8:]), {7: 0}
        operands.append(earlier)
    return pl.pallas_call(
        kernel,
        grid_spec=pltpu.PrefetchScalarGridSpec(
            num_scalar_prefetch=1,
            grid=(high - low,),
            in_specs=[any_spec()] * 3 + [whole(flip), whole(mask), whole(base)] + [any_spec()] * (len(operands) - 7),
            out_specs=pl.BlockSpec((1, buffer_rows, width, chans), lambda e, m: (e + low, 0, 0, 0)),
            scratch_shapes=[
                pltpu.VMEM((2, buffer_rows, width, chans), BF16),
                pltpu.VMEM((2, height, width, chans), BF16),
                pltpu.VMEM((target_rows, width, chans), BF16),
                pltpu.VMEM((rows * width, 2 * chans), BF16),
                pltpu.SemaphoreType.DMA((2, 2)),
            ],
        ),
        out_shape=jax.ShapeDtypeStruct((edges, buffer_rows, width, chans), BF16),
        input_output_aliases=aliases,
        compiler_params=pltpu.CompilerParams(vmem_limit_bytes=VMEM_LIMIT),
        cost_estimate=pl.CostEstimate(
            flops=8 * (high - low) * height * width * chans * rows * width,
            bytes_accessed=6 * (high - low) * height * width * chans,
            transcendentals=0,
        ),
        name=f"motion_from{low}",
    )(*operands)


def gru_kernel(
    first,
    last,
    meta,
    own,
    near,
    far,
    motion,
    gates,
    state,
    w_input,
    w_candidate,
    _,
    new_ref,
    own_sum,
    far_sum,
    near_top,
    near_low,
    ctx_buf,
    motion_buf,
    gates_buf,
    state_buf,
    columns,
    update_buf,
    drive_buf,
    totals,
    sems,
):
    edge = pl.program_id(0)
    edges = pl.num_programs(0)
    frames = own.shape[0]
    height, width, chans = own.shape[2:]
    slot = lax.rem(edge, 2)
    top = max(first - 1, 0)
    end = min(last + 1, height)
    rows = end - top

    def start(e, s):
        buf, frame = meta[e, 0], meta[e, 1]
        pltpu.make_async_copy(motion.at[e, pl.ds(top + 1, rows)], motion_buf.at[s], sems.at[1, s]).start()
        pltpu.make_async_copy(gates.at[e, pl.ds(top, rows)], gates_buf.at[s], sems.at[2, s]).start()
        pltpu.make_async_copy(state.at[e, pl.ds(top, rows)], state_buf.at[s], sems.at[3, s]).start()
        cases = (
            (buf == 0, own.at[frame, 1, pl.ds(top, rows)]),
            (buf == 1, far.at[frame, pl.ds(top, rows)]),
            (buf == 2, near.at[frame, 1, pl.ds(top, rows)]),
        )
        fetch(cases, ctx_buf.at[s], sems.at[0, s])

    def finish(s):
        await_copy(motion_buf.at[s], sems.at[1, s])
        await_copy(gates_buf.at[s], sems.at[2, s])
        await_copy(state_buf.at[s], sems.at[3, s])
        await_copy(ctx_buf.at[s], sems.at[0, s])

    @pl.when(edge == 0)
    def _():
        start(edge, slot)
        edge_row = jnp.zeros((1,) + columns.shape[1:], BF16)
        columns[0:1] = edge_row
        columns[rows + 1 :] = edge_row
        totals[...] = jnp.zeros(totals.shape, F32)

    @pl.when(edge + 1 < edges)
    def _():
        start(edge + 1, 1 - slot)

    finish(slot)

    weights = w_input[...]
    step = 5
    for y in range(0, rows, step):
        count = min(step, rows - y)
        span = slice(y, y + count)
        mixed = jnp.concatenate([motion_buf[slot, span], ctx_buf[slot, span]], axis=-1)
        inputs = jnp.dot(mixed.reshape(count * width, 2 * chans), weights, preferred_element_type=F32)
        inputs = inputs.reshape(count, width, 3 * chans)
        pre = gates_buf[slot, span].astype(F32)
        update_buf[span] = sigmoid(pre[..., :chans] + inputs[..., :chans])
        reset = sigmoid(pre[..., chans:] + inputs[..., chans : 2 * chans])
        drive_buf[span] = inputs[..., 2 * chans :]
        held = (reset * state_buf[slot, span].astype(F32)).astype(BF16).astype(F32)
        put_columns(columns, y + 1, held)

    weights = w_candidate[...]
    place = meta[edge, 0] * frames + meta[edge, 1]
    step = 8
    for y in range(first, last, step):
        count = min(step, last - y)
        span = slice(y - top, y - top + count)
        conv = conv_rows(columns, y - top, count, weights).reshape(count, width, chans)
        candidate = jnp.tanh(conv + drive_buf[span])
        update = update_buf[span]
        fresh = ((1.0 - update) * state_buf[slot, span].astype(F32) + update * candidate).astype(BF16)
        new_ref[0, y - first : y - first + count] = fresh
        totals[place, y - first : y - first + count] += fresh.astype(F32)

    @pl.when(edge == edges - 1)
    def _():
        half = near_top.shape[1]
        own_sum[...] = totals[:frames].astype(BF16)
        far_sum[...] = totals[frames : 2 * frames].astype(BF16)
        near_top[...] = totals[2 * frames :, :half].astype(BF16)
        near_low[...] = totals[2 * frames :, half:].astype(BF16)


def gru_of(band, meta, own, near, far, motion, gates, state, w_input, w_candidate, earlier):
    frames, _, height, width, chans = own.shape
    edges = state.shape[0]
    size = height // 2
    first, last = band * size, (band + 1) * size
    rows = min(last + 1, height) - max(first - 1, 0)
    sums = jax.ShapeDtypeStruct((frames, size, width, chans), BF16)
    pieces = jax.ShapeDtypeStruct((frames, size // 2, width, chans), BF16)
    sum_spec = pl.BlockSpec(sums.shape, lambda e, m: (0, 0, 0, 0))
    piece_spec = pl.BlockSpec(pieces.shape, lambda e, m: (0, 0, 0, 0))
    body = functools.partial(gru_kernel, first, last)
    operands = [meta, own, near, far, motion, gates, state, w_input, w_candidate]
    if earlier is None:
        kernel = lambda *refs: body(*refs[:9], None, *refs[9:])
        aliases = {}
    else:
        kernel = body
        operands.append(earlier)
        aliases = {9: 0}
    return pl.pallas_call(
        kernel,
        grid_spec=pltpu.PrefetchScalarGridSpec(
            num_scalar_prefetch=1,
            grid=(edges,),
            in_specs=[any_spec()] * 6 + [whole(w_input), whole(w_candidate)] + [any_spec()] * (len(operands) - 9),
            out_specs=[
                pl.BlockSpec((1, size, width, chans), lambda e, m: (e, band, 0, 0)),
                sum_spec,
                sum_spec,
                piece_spec,
                piece_spec,
            ],
            scratch_shapes=[
                pltpu.VMEM((2, rows, width, chans), BF16),
                pltpu.VMEM((2, rows, width, chans), BF16),
                pltpu.VMEM((2, rows, width, 2 * chans), BF16),
                pltpu.VMEM((2, rows, width, chans), BF16),
                pltpu.VMEM((rows + 2, width, 3 * chans), BF16),
                pltpu.VMEM((rows, width, chans), F32),
                pltpu.VMEM((rows, width, chans), F32),
                pltpu.VMEM((3 * frames, size, width, chans), F32),
                pltpu.SemaphoreType.DMA((4, 2)),
            ],
        ),
        out_shape=[
            jax.ShapeDtypeStruct(state.shape, BF16),
            sums,
            sums,
            pieces,
            pieces,
        ],
        input_output_aliases=aliases,
        compiler_params=pltpu.CompilerParams(vmem_limit_bytes=VMEM_LIMIT),
        cost_estimate=pl.CostEstimate(
            flops=2 * edges * rows * width * chans * (6 * chans + 9 * chans),
            bytes_accessed=2 * edges * rows * width * chans * 6,
            transcendentals=3 * edges * rows * width * chans,
        ),
        name=f"gru_band{band}",
    )(*operands)


def aggregate_kernel(pieces, first, last, counts, *refs):
    sums, weights_ref, rest = refs[: 4 * len(pieces)], refs[4 * len(pieces)], refs[4 * len(pieces) + 1 :]
    out_ref, columns = rest[-2:]
    width, chans = out_ref.shape[2:]
    edge_row = jnp.zeros((1,) + columns.shape[1:], BF16)
    columns[0:1] = edge_row
    columns[columns.shape[0] - 1 :] = edge_row
    count = counts[pl.program_id(0)]
    at = 1
    for i, (low, high) in enumerate(pieces):
        own, far, *near = sums[4 * i : 4 * i + 4]
        half = near[0].shape[1]
        for k in range(2):
            top, end = max(low - k * half, 0), min(high - k * half, half)
            if end > top:
                span = slice(k * half + top, k * half + end)
                total = own[0, span].astype(F32) + far[0, span].astype(F32) + near[k][0, top:end].astype(F32)
                mean = (total / count).astype(BF16).astype(F32)
                put_columns(columns, at, mean)
                at += end - top
    step = 8
    base = 0
    if len(rest) == 3:
        out_ref[0, :first] = rest[0][0]
        base = first
    weights = weights_ref[...]
    skip = 0 if first == 0 else 1
    for y in range(0, last - first, step):
        rows = min(step, last - first - y)
        out = conv_rows(columns, y + skip, rows, weights)
        out_ref[0, base + y : base + y + rows] = out.astype(BF16).reshape(rows, width, chans)


def aggregate_of(first, last, pieces, bands, counts, weights, earlier):
    frames, _, width, chans = bands[0][0].shape
    sums = [array for band in bands for array in band]
    depth = sum(high - low for low, high in pieces)
    rows = last if earlier is not None else last - first
    operands = [counts, *sums, weights]
    more = []
    if earlier is not None:
        operands.append(earlier)
        more = [pl.BlockSpec((1,) + earlier.shape[1:], lambda f, c: (f, 0, 0, 0))]
    return pl.pallas_call(
        functools.partial(aggregate_kernel, pieces, first, last),
        grid_spec=pltpu.PrefetchScalarGridSpec(
            num_scalar_prefetch=1,
            grid=(frames,),
            in_specs=[pl.BlockSpec((1,) + array.shape[1:], lambda f, c: (f, 0, 0, 0)) for array in sums]
            + [whole(weights)]
            + more,
            out_specs=pl.BlockSpec((1, rows, width, chans), lambda f, c: (f, 0, 0, 0)),
            scratch_shapes=[pltpu.VMEM((depth + 2, width, 3 * chans), BF16)],
        ),
        out_shape=jax.ShapeDtypeStruct((frames, rows, width, chans), BF16),
        compiler_params=pltpu.CompilerParams(vmem_limit_bytes=16 << 20),
        cost_estimate=pl.CostEstimate(
            flops=2 * frames * (last - first) * width * 9 * chans * chans,
            bytes_accessed=8 * frames * depth * width * chans,
            transcendentals=0,
        ),
        name=f"aggregate_from{first}",
    )(*operands)


def per_device(
    frame_maps, net_state, edges, offsets, w_motion, w_input, w_gates, w_candidate, w_aggregate
):
    frames, _, height, width, chans = frame_maps.shape
    edge_count = net_state.shape[0]
    me = lax.axis_index("rows")
    count = lax.axis_size("rows")
    near_route = [(i, i ^ 1) for i in range(count)]
    far_route = [(i, i + 1 if i % 2 else i - 1) for i in range(1, count - 1)]

    def far_swap(block, *after):
        if after:
            block = lax.optimization_barrier((block,) + after)[0]
        return lax.ppermute(block, "rows", far_route)

    def near_swap(block):
        return lax.ppermute(block, "rows", near_route)

    far_feat = far_swap(frame_maps[:, 0])
    near = near_swap(frame_maps)

    my_edges = lax.dynamic_slice_in_dim(edges, me * edge_count, edge_count, 0)
    owner = my_edges // frames
    buf = jnp.where(owner == me, 0, jnp.where(owner == (me ^ 1), 2, 1))
    local = my_edges % frames
    meta = jnp.stack(
        [buf[:, 0], local[:, 0], buf[:, 1], local[:, 1], offsets[:, 0], offsets[:, 1]], axis=1
    ).astype(jnp.int32)
    mine = me * frames + jnp.arange(frames, dtype=jnp.int32)
    counts = jnp.maximum(jnp.sum((edges[:, 0][:, None] == mine[None]).astype(F32), axis=0), 1.0)

    base = motion_weights(w_motion, width)
    gates = gates_of(net_state, lax.optimization_barrier((w_gates, near))[0])
    half = edge_count // 2
    held_meta = lax.optimization_barrier((meta, gates))[0]
    motion = motion_of(0, half, held_meta, frame_maps, near, far_feat, base, None)
    context = lax.optimization_barrier((frame_maps, near))[0][:, 1]
    far_ctx = far_swap(context, motion)
    motion = motion_of(half, edge_count, meta, frame_maps, near, far_feat, base, motion)
    maps = (meta, frame_maps, near, far_ctx, motion, gates, net_state, w_input, w_candidate)

    new_state, own_first, far_sum, *near_first = gru_of(0, *maps, None)
    far_first = far_swap(far_sum)
    new_state, own_second, far_sum, *near_second = gru_of(1, *maps, new_state)
    far_second = far_swap(far_sum, far_first)
    near_first, near_second = (
        [near_swap(piece) for piece in lax.optimization_barrier((*pieces, far_first))[:2]]
        for pieces in (near_first, near_second)
    )
    first = (own_first, far_first, *near_first)
    second = (own_second, far_second, *near_second)
    size = height // 2
    upper = aggregate_of(0, size - 1, ((0, size),), (first,), counts, w_aggregate, None)
    frame_update = aggregate_of(
        size - 1, height, ((size - 2, size), (0, size)), (first, second), counts, w_aggregate, upper
    )
    return (new_state, frame_update)


def solution(mesh):
    in_specs = (
        P(("groups", "rows"), None, None, None, None),
        P(("groups", "rows"), None, None, None),
        P("groups", None),
        P(("groups", "rows"), None),
        P(),
        P(),
        P(),
        P(),
        P(),
    )
    out_specs = (P(("groups", "rows"), None, None, None), P(("groups", "rows"), None, None, None))
    return jax.shard_map(
        per_device, mesh=mesh, in_specs=in_specs, out_specs=out_specs, check_vma=False
    )
```

```python
import functools

import jax
import jax.numpy as jnp
import numpy as np
from jax import lax
from jax.experimental import pallas as pl
from jax.experimental.pallas import tpu as pltpu
from jax.sharding import PartitionSpec as P

RADIUS = 4
SHIFT = 8
SPAN = 2 * RADIUS + 1
MARGIN = SHIFT + RADIUS
F32 = jnp.float32
BF16 = jnp.bfloat16
VMEM_LIMIT = 60 << 20


def any_spec():
    return pl.BlockSpec(memory_space=pl.ANY)


def whole(array):
    return pl.BlockSpec(array.shape, lambda *_: (0,) * array.ndim)


def fetch(cases, dst, sem):
    for condition, src in cases:

        @pl.when(condition)
        def _(src=src):
            pltpu.make_async_copy(src, dst, sem).start()


def await_copy(dst, sem):
    pltpu.make_async_copy(dst, dst, sem).wait()


def neighbours(block):
    rows, width, chans = block.shape
    flat = block.reshape(rows * width, chans)
    x = lax.broadcasted_iota(jnp.int32, (rows, width, chans), 1).reshape(rows * width, chans)
    left = jnp.where(x == 0, 0.0, pltpu.roll(flat, 1, 0)).astype(BF16)
    right = jnp.where(x == width - 1, 0.0, pltpu.roll(flat, rows * width - 1, 0)).astype(BF16)
    return [side.reshape(rows, width, chans) for side in (left, flat.astype(BF16), right)]


def put_columns(columns, start, block):
    chans = block.shape[-1]
    rows = block.shape[0]
    for i, side in enumerate(neighbours(block)):
        columns[pl.ds(start, rows), :, i * chans : (i + 1) * chans] = side


def conv_rows(columns, start, rows, weights):
    width, depth = columns.shape[1:]
    taps = [columns[pl.ds(start + step, rows)].reshape(rows * width, depth) for step in range(3)]
    return jnp.dot(jnp.concatenate(taps, axis=1), weights, preferred_element_type=F32)


def sigmoid(v):
    return 0.5 * jnp.tanh(0.5 * v) + 0.5


def gates_kernel(state_ref, weights_ref, out_ref, columns):
    height, width, chans = state_ref.shape[1:]
    edge_row = jnp.zeros((1,) + columns.shape[1:], BF16)
    columns[0:1] = edge_row
    columns[height + 1 :] = edge_row
    step = 8
    for y in range(0, height, step):
        put_columns(columns, y + 1, state_ref[0, y : y + step].astype(F32))
    weights = weights_ref[...]
    for y in range(0, height, step):
        gates = conv_rows(columns, y, step, weights)
        out_ref[0, y : y + step] = gates.astype(BF16).reshape(step, width, weights.shape[1])


def gates_of(state, weights):
    edges, height, width, chans = state.shape
    outs = weights.shape[1]
    return pl.pallas_call(
        gates_kernel,
        grid=(edges,),
        in_specs=[pl.BlockSpec((1, height, width, chans), lambda e: (e, 0, 0, 0)), whole(weights)],
        out_specs=pl.BlockSpec((1, height, width, outs), lambda e: (e, 0, 0, 0)),
        out_shape=jax.ShapeDtypeStruct((edges, height, width, outs), BF16),
        scratch_shapes=[pltpu.VMEM((height + 2, width, 3 * chans), BF16)],
        compiler_params=pltpu.CompilerParams(vmem_limit_bytes=VMEM_LIMIT),
        cost_estimate=pl.CostEstimate(
            flops=2 * edges * height * width * 9 * chans * outs,
            bytes_accessed=2 * edges * height * width * (chans + outs),
            transcendentals=0,
        ),
        name="gates",
    )(state, weights)


def motion_kernel(low, meta, own, near, far, flip_ref, mask_ref, base_ref, out_ref, src_buf, raw_buf, tgt_buf, w_buf, sems):
    step = pl.program_id(0)
    steps = pl.num_programs(0)
    edge = step + low
    height, width, chans = own.shape[2:]
    slot = lax.rem(step, 2)
    lanes = 2 * width
    tiles = base_ref.shape[0]

    def start(e, s):
        def cases(buf, frame):
            return ((buf == 0, own.at[frame, 0]), (buf == 1, far.at[frame]), (buf == 2, near.at[frame, 0]))

        fetch(cases(meta[e, 0], meta[e, 1]), src_buf.at[s, pl.ds(1, height)], sems.at[0, s])
        fetch(cases(meta[e, 2], meta[e, 3]), raw_buf.at[s], sems.at[1, s])

    @pl.when(step == 0)
    def _():
        start(edge, slot)
        tgt_buf[0:MARGIN] = jnp.zeros((MARGIN, width, chans), BF16)
        below = tgt_buf.shape[0] - MARGIN - height
        tgt_buf[MARGIN + height :] = jnp.zeros((below, width, chans), BF16)

    @pl.when(step + 1 < steps)
    def _():
        start(edge + 1, 1 - slot)

    oy, ox = meta[edge, 4], meta[edge, 5]
    for j in range(tiles):
        w_buf[j * lanes : (j + 1) * lanes] = pltpu.roll(base_ref[j], lax.rem(lanes - ox, lanes), 0).astype(BF16)

    await_copy(src_buf.at[slot, pl.ds(1, height)], sems.at[0, slot])
    await_copy(raw_buf.at[slot], sems.at[1, slot])

    flip = flip_ref[...]
    for y in range(0, height, 2):
        block = raw_buf[slot, y : y + 2].reshape(lanes, chans)
        turned = jnp.dot(flip, block, preferred_element_type=F32).astype(BF16)
        tgt_buf[MARGIN + y : MARGIN + y + 2] = turned.reshape(2, width, chans)

    mask = mask_ref[...]
    keep = mask != 0.0
    odd = lax.rem(oy + 2 * SHIFT, 2)
    weights = w_buf[...]
    unroll = 5

    @pl.loop(0, (height // 2 + unroll) // unroll)
    def _(i):
        starts = [2 * (i * unroll + u) - odd for u in range(unroll)]
        scores = []
        for y in starts:
            lhs = src_buf[slot, pl.ds(y + 1, 2)].reshape(lanes, chans)
            rhs = tgt_buf[pl.ds(y + oy - RADIUS + MARGIN, 2 * tiles)].reshape(tiles * lanes, chans)
            scores.append(lax.dot_general(lhs, rhs, (((1,), (1,)), ((), ())), preferred_element_type=F32))
        for y, pair in zip(starts, scores):
            volume = []
            for r in range(2):
                parts = []
                for j in range(tiles):
                    tile = pair[r * width : (r + 1) * width, j * lanes : (j + 1) * lanes] * (chans**-0.5)
                    tile = pltpu.roll(tile.astype(BF16), 0, 1, stride=1, stride_axis=0)
                    parts.append(jnp.where(keep, tile.astype(F32), 0.0).astype(BF16))
                volume.append(jnp.concatenate(parts, axis=1))
            res = jnp.dot(jnp.concatenate(volume, axis=0), weights, preferred_element_type=F32)
            out_ref[0, pl.ds(y + 1, 1)] = jnp.maximum(res[:width, :chans], 0.0).astype(BF16)[None]
            out_ref[0, pl.ds(y + 2, 1)] = jnp.maximum(res[width:, chans:], 0.0).astype(BF16)[None]


def motion_constants(width, chans):
    lanes = 2 * width
    rows = SPAN + 1
    place = np.zeros((2, rows // 2, lanes, SPAN * SPAN), np.float32)
    for r in range(rows):
        for b in range(SPAN):
            lane = (width - 1 + RADIUS - b + width * (r % 2)) % lanes
            for parity in range(2):
                if 0 <= r - parity < SPAN:
                    place[parity, r // 2, lane, (r - parity) * SPAN + b] = 1.0
    flip = np.kron(np.eye(2), np.eye(width)[::-1])
    x = np.arange(width)[:, None]
    lane = np.arange(lanes)[None]
    middle = (lane >= width // 2) & (lane < width + width // 2)
    inside = np.where(middle, (lane >= x) & (lane < x + width), np.where(lane < width, x > lane, lane >= x + width))
    return place.astype(BF16), flip.astype(BF16), inside.astype(np.float32)


def motion_weights(w_motion, width):
    place = motion_constants(width, w_motion.shape[1])[0]
    return jnp.concatenate(
        [jnp.einsum("tlk,kc->tlc", side, w_motion, preferred_element_type=F32) for side in place], axis=2
    )


def motion_of(low, high, meta, own, near, far, base, earlier):
    _, _, height, width, chans = own.shape
    edges = meta.shape[0]
    rows = SPAN + 1
    _, flip, mask = motion_constants(width, chans)
    buffer_rows = height + 4
    target_rows = height + 2 * MARGIN + 2
    operands = [meta, own, near, far, flip, mask, base]
    body = functools.partial(motion_kernel, low)
    if earlier is None:
        kernel, aliases = body, {}
    else:
        kernel, aliases = lambda *refs: body(*refs[:7], *refs[8:]), {7: 0}
        operands.append(earlier)
    return pl.pallas_call(
        kernel,
        grid_spec=pltpu.PrefetchScalarGridSpec(
            num_scalar_prefetch=1,
            grid=(high - low,),
            in_specs=[any_spec()] * 3 + [whole(flip), whole(mask), whole(base)] + [any_spec()] * (len(operands) - 7),
            out_specs=pl.BlockSpec((1, buffer_rows, width, chans), lambda e, m: (e + low, 0, 0, 0)),
            scratch_shapes=[
                pltpu.VMEM((2, buffer_rows, width, chans), BF16),
                pltpu.VMEM((2, height, width, chans), BF16),
                pltpu.VMEM((target_rows, width, chans), BF16),
                pltpu.VMEM((rows * width, 2 * chans), BF16),
                pltpu.SemaphoreType.DMA((2, 2)),
            ],
        ),
        out_shape=jax.ShapeDtypeStruct((edges, buffer_rows, width, chans), BF16),
        input_output_aliases=aliases,
        compiler_params=pltpu.CompilerParams(vmem_limit_bytes=VMEM_LIMIT),
        cost_estimate=pl.CostEstimate(
            flops=8 * (high - low) * height * width * chans * rows * width,
            bytes_accessed=6 * (high - low) * height * width * chans,
            transcendentals=0,
        ),
        name=f"motion_from{low}",
    )(*operands)


def gru_kernel(
    first,
    last,
    meta,
    own,
    near,
    far_top,
    far_low,
    motion,
    gates,
    state,
    w_input,
    w_candidate,
    _,
    new_ref,
    own_sum,
    far_sum,
    near_top,
    near_low,
    ctx_buf,
    motion_buf,
    gates_buf,
    state_buf,
    columns,
    update_buf,
    drive_buf,
    totals,
    sems,
):
    edge = pl.program_id(0)
    edges = pl.num_programs(0)
    frames = own.shape[0]
    height, width, chans = own.shape[2:]
    slot = lax.rem(edge, 2)
    top = max(first - 1, 0)
    end = min(last + 1, height)
    rows = end - top
    split = far_top.shape[1]
    above = min(split - top, rows)
    context_pieces = [
        piece for piece in ((far_top, 0, above, 0), (far_low, above, rows, 4)) if piece[2] > piece[1]
    ]

    def start(e, s):
        buf, frame = meta[e, 0], meta[e, 1]
        pltpu.make_async_copy(motion.at[e, pl.ds(top + 1, rows)], motion_buf.at[s], sems.at[1, s]).start()
        pltpu.make_async_copy(gates.at[e, pl.ds(top, rows)], gates_buf.at[s], sems.at[2, s]).start()
        pltpu.make_async_copy(state.at[e, pl.ds(top, rows)], state_buf.at[s], sems.at[3, s]).start()
        for far, low, high, sem in context_pieces:
            cases = (
                (buf == 0, own.at[frame, 1, pl.ds(top + low, high - low)]),
                (buf == 1, far.at[frame, pl.ds(top + low - (0 if far is far_top else split), high - low)]),
                (buf == 2, near.at[frame, 1, pl.ds(top + low, high - low)]),
            )
            fetch(cases, ctx_buf.at[s, pl.ds(low, high - low)], sems.at[sem, s])

    def finish(s):
        await_copy(motion_buf.at[s], sems.at[1, s])
        await_copy(gates_buf.at[s], sems.at[2, s])
        await_copy(state_buf.at[s], sems.at[3, s])
        for _, low, high, sem in context_pieces:
            await_copy(ctx_buf.at[s, pl.ds(low, high - low)], sems.at[sem, s])

    @pl.when(edge == 0)
    def _():
        start(edge, slot)
        edge_row = jnp.zeros((1,) + columns.shape[1:], BF16)
        columns[0:1] = edge_row
        columns[rows + 1 :] = edge_row
        totals[...] = jnp.zeros(totals.shape, F32)

    @pl.when(edge + 1 < edges)
    def _():
        start(edge + 1, 1 - slot)

    finish(slot)

    weights = w_input[...]
    step = 5
    for y in range(0, rows, step):
        count = min(step, rows - y)
        span = slice(y, y + count)
        mixed = jnp.concatenate([motion_buf[slot, span], ctx_buf[slot, span]], axis=-1)
        inputs = jnp.dot(mixed.reshape(count * width, 2 * chans), weights, preferred_element_type=F32)
        inputs = inputs.reshape(count, width, 3 * chans)
        pre = gates_buf[slot, span].astype(F32)
        update_buf[span] = sigmoid(pre[..., :chans] + inputs[..., :chans])
        reset = sigmoid(pre[..., chans:] + inputs[..., chans : 2 * chans])
        drive_buf[span] = inputs[..., 2 * chans :]
        held = (reset * state_buf[slot, span].astype(F32)).astype(BF16).astype(F32)
        put_columns(columns, y + 1, held)

    weights = w_candidate[...]
    place = meta[edge, 0] * frames + meta[edge, 1]
    step = 8
    for y in range(first, last, step):
        count = min(step, last - y)
        span = slice(y - top, y - top + count)
        conv = conv_rows(columns, y - top, count, weights).reshape(count, width, chans)
        candidate = jnp.tanh(conv + drive_buf[span])
        update = update_buf[span]
        fresh = ((1.0 - update) * state_buf[slot, span].astype(F32) + update * candidate).astype(BF16)
        new_ref[0, y - first : y - first + count] = fresh
        totals[place, y - first : y - first + count] += fresh.astype(F32)

    @pl.when(edge == edges - 1)
    def _():
        half = near_top.shape[1]
        own_sum[...] = totals[:frames].astype(BF16)
        far_sum[...] = totals[frames : 2 * frames].astype(BF16)
        near_top[...] = totals[2 * frames :, :half].astype(BF16)
        near_low[...] = totals[2 * frames :, half:].astype(BF16)


def gru_of(band, meta, own, near, far_top, far_low, motion, gates, state, w_input, w_candidate, earlier):
    frames, _, height, width, chans = own.shape
    edges = state.shape[0]
    size = height // 2
    first, last = band * size, (band + 1) * size
    rows = min(last + 1, height) - max(first - 1, 0)
    sums = jax.ShapeDtypeStruct((frames, size, width, chans), BF16)
    pieces = jax.ShapeDtypeStruct((frames, size // 2, width, chans), BF16)
    sum_spec = pl.BlockSpec(sums.shape, lambda e, m: (0, 0, 0, 0))
    piece_spec = pl.BlockSpec(pieces.shape, lambda e, m: (0, 0, 0, 0))
    body = functools.partial(gru_kernel, first, last)
    operands = [meta, own, near, far_top, far_low, motion, gates, state, w_input, w_candidate]
    if earlier is None:
        kernel = lambda *refs: body(*refs[:10], None, *refs[10:])
        aliases = {}
    else:
        kernel = body
        operands.append(earlier)
        aliases = {10: 0}
    return pl.pallas_call(
        kernel,
        grid_spec=pltpu.PrefetchScalarGridSpec(
            num_scalar_prefetch=1,
            grid=(edges,),
            in_specs=[any_spec()] * 7 + [whole(w_input), whole(w_candidate)] + [any_spec()] * (len(operands) - 10),
            out_specs=[
                pl.BlockSpec((1, size, width, chans), lambda e, m: (e, band, 0, 0)),
                sum_spec,
                sum_spec,
                piece_spec,
                piece_spec,
            ],
            scratch_shapes=[
                pltpu.VMEM((2, rows, width, chans), BF16),
                pltpu.VMEM((2, rows, width, chans), BF16),
                pltpu.VMEM((2, rows, width, 2 * chans), BF16),
                pltpu.VMEM((2, rows, width, chans), BF16),
                pltpu.VMEM((rows + 2, width, 3 * chans), BF16),
                pltpu.VMEM((rows, width, chans), F32),
                pltpu.VMEM((rows, width, chans), F32),
                pltpu.VMEM((3 * frames, size, width, chans), F32),
                pltpu.SemaphoreType.DMA((5, 2)),
            ],
        ),
        out_shape=[
            jax.ShapeDtypeStruct(state.shape, BF16),
            sums,
            sums,
            pieces,
            pieces,
        ],
        input_output_aliases=aliases,
        compiler_params=pltpu.CompilerParams(vmem_limit_bytes=VMEM_LIMIT),
        cost_estimate=pl.CostEstimate(
            flops=2 * edges * rows * width * chans,
            bytes_accessed=2 * edges * rows * width * chans,
            transcendentals=0,
        ),
        name=f"gru_band{band}",
    )(*operands)


def aggregate_kernel(pieces, first, last, counts, *refs):
    sums, weights_ref, rest = refs[: 4 * len(pieces)], refs[4 * len(pieces)], refs[4 * len(pieces) + 1 :]
    out_ref, columns = rest[-2:]
    width, chans = out_ref.shape[2:]
    edge_row = jnp.zeros((1,) + columns.shape[1:], BF16)
    columns[0:1] = edge_row
    columns[columns.shape[0] - 1 :] = edge_row
    count = counts[pl.program_id(0)]
    at = 1
    for i, (low, high) in enumerate(pieces):
        own, far, *near = sums[4 * i : 4 * i + 4]
        half = near[0].shape[1]
        for k in range(2):
            top, end = max(low - k * half, 0), min(high - k * half, half)
            if end > top:
                span = slice(k * half + top, k * half + end)
                total = own[0, span].astype(F32) + far[0, span].astype(F32) + near[k][0, top:end].astype(F32)
                mean = (total / count).astype(BF16).astype(F32)
                put_columns(columns, at, mean)
                at += end - top
    step = 8
    base = 0
    if len(rest) == 3:
        out_ref[0, :first] = rest[0][0]
        base = first
    weights = weights_ref[...]
    skip = 0 if first == 0 else 1
    for y in range(0, last - first, step):
        rows = min(step, last - first - y)
        out = conv_rows(columns, y + skip, rows, weights)
        out_ref[0, base + y : base + y + rows] = out.astype(BF16).reshape(rows, width, chans)


def aggregate_of(first, last, pieces, bands, counts, weights, earlier):
    frames, _, width, chans = bands[0][0].shape
    sums = [array for band in bands for array in band]
    depth = sum(high - low for low, high in pieces)
    rows = last if earlier is not None else last - first
    operands = [counts, *sums, weights]
    more = []
    if earlier is not None:
        operands.append(earlier)
        more = [pl.BlockSpec((1,) + earlier.shape[1:], lambda f, c: (f, 0, 0, 0))]
    return pl.pallas_call(
        functools.partial(aggregate_kernel, pieces, first, last),
        grid_spec=pltpu.PrefetchScalarGridSpec(
            num_scalar_prefetch=1,
            grid=(frames,),
            in_specs=[pl.BlockSpec((1,) + array.shape[1:], lambda f, c: (f, 0, 0, 0)) for array in sums]
            + [whole(weights)]
            + more,
            out_specs=pl.BlockSpec((1, rows, width, chans), lambda f, c: (f, 0, 0, 0)),
            scratch_shapes=[pltpu.VMEM((depth + 2, width, 3 * chans), BF16)],
        ),
        out_shape=jax.ShapeDtypeStruct((frames, rows, width, chans), BF16),
        compiler_params=pltpu.CompilerParams(vmem_limit_bytes=16 << 20),
        cost_estimate=pl.CostEstimate(
            flops=2 * frames * (last - first) * width * 9 * chans * chans,
            bytes_accessed=8 * frames * depth * width * chans,
            transcendentals=0,
        ),
        name=f"aggregate_from{first}",
    )(*operands)


def per_device(
    frame_maps, net_state, edges, offsets, w_motion, w_input, w_gates, w_candidate, w_aggregate
):
    frames, _, height, width, chans = frame_maps.shape
    edge_count = net_state.shape[0]
    me = lax.axis_index("rows")
    count = lax.axis_size("rows")
    near_route = [(i, i ^ 1) for i in range(count)]
    far_route = [(i, i + 1 if i % 2 else i - 1) for i in range(1, count - 1)]

    def far_swap(block, *after):
        if after:
            block = lax.optimization_barrier((block,) + after)[0]
        return lax.ppermute(block, "rows", far_route)

    def near_swap(block):
        return lax.ppermute(block, "rows", near_route)

    far_feat = far_swap(frame_maps[:, 0])
    near = near_swap(frame_maps)

    my_edges = lax.dynamic_slice_in_dim(edges, me * edge_count, edge_count, 0)
    owner = my_edges // frames
    buf = jnp.where(owner == me, 0, jnp.where(owner == (me ^ 1), 2, 1))
    local = my_edges % frames
    meta = jnp.stack(
        [buf[:, 0], local[:, 0], buf[:, 1], local[:, 1], offsets[:, 0], offsets[:, 1]], axis=1
    ).astype(jnp.int32)
    mine = me * frames + jnp.arange(frames, dtype=jnp.int32)
    counts = jnp.maximum(jnp.sum((edges[:, 0][:, None] == mine[None]).astype(F32), axis=0), 1.0)

    base = motion_weights(w_motion, width)
    gates = gates_of(net_state, lax.optimization_barrier((w_gates, near))[0])
    half = edge_count // 2
    held_meta = lax.optimization_barrier((meta, gates))[0]
    motion = motion_of(0, half, held_meta, frame_maps, near, far_feat, base, None)
    context = lax.optimization_barrier((frame_maps, near))[0][:, 1]
    split = height // 2 + 1
    far_top = far_swap(context[:, :split], motion)
    far_low = far_swap(context[:, split:], motion)
    motion = motion_of(half, edge_count, meta, frame_maps, near, far_feat, base, motion)

    def gru(band, earlier):
        fars = (far_top, far_low if band else far_top)
        return gru_of(band, meta, frame_maps, near, *fars, motion, gates, net_state, w_input, w_candidate, earlier)

    new_state, own_first, far_sum, *near_first = gru(0, None)
    far_first = far_swap(far_sum)
    new_state, own_second, far_sum, *near_second = gru(1, new_state)
    far_second = far_swap(far_sum)
    near_first, near_second = (
        [near_swap(piece) for piece in lax.optimization_barrier((*pieces, far_first))[:2]]
        for pieces in (near_first, near_second)
    )
    first = (own_first, far_first, *near_first)
    second = (own_second, far_second, *near_second)
    size = height // 2
    upper = aggregate_of(0, size - 1, ((0, size),), (first,), counts, w_aggregate, None)
    frame_update = aggregate_of(
        size - 1, height, ((size - 2, size), (0, size)), (first, second), counts, w_aggregate, upper
    )
    return (new_state, frame_update)


def solution(mesh):
    in_specs = (
        P(("groups", "rows"), None, None, None, None),
        P(("groups", "rows"), None, None, None),
        P("groups", None),
        P(("groups", "rows"), None),
        P(),
        P(),
        P(),
        P(),
        P(),
    )
    out_specs = (P(("groups", "rows"), None, None, None), P(("groups", "rows"), None, None, None))
    return jax.shard_map(
        per_device, mesh=mesh, in_specs=in_specs, out_specs=out_specs, check_vma=False
    )
```

```python
import functools

import jax
import jax.numpy as jnp
import numpy as np
from jax import lax
from jax.experimental import pallas as pl
from jax.experimental.pallas import tpu as pltpu
from jax.sharding import PartitionSpec as P

RADIUS = 4
SHIFT = 8
SPAN = 2 * RADIUS + 1
MARGIN = SHIFT + RADIUS
F32 = jnp.float32
BF16 = jnp.bfloat16
VMEM_LIMIT = 60 << 20


def any_spec():
    return pl.BlockSpec(memory_space=pl.ANY)


def whole(array):
    return pl.BlockSpec(array.shape, lambda *_: (0,) * array.ndim)


def fetch(cases, dst, sem):
    for condition, src in cases:

        @pl.when(condition)
        def _(src=src):
            pltpu.make_async_copy(src, dst, sem).start()


def await_copy(dst, sem):
    pltpu.make_async_copy(dst, dst, sem).wait()


def neighbours(block):
    rows, width, chans = block.shape
    flat = block.reshape(rows * width, chans)
    x = lax.broadcasted_iota(jnp.int32, (rows, width, chans), 1).reshape(rows * width, chans)
    left = jnp.where(x == 0, 0.0, pltpu.roll(flat, 1, 0)).astype(BF16)
    right = jnp.where(x == width - 1, 0.0, pltpu.roll(flat, rows * width - 1, 0)).astype(BF16)
    return [side.reshape(rows, width, chans) for side in (left, flat.astype(BF16), right)]


def put_columns(columns, start, block):
    chans = block.shape[-1]
    rows = block.shape[0]
    for i, side in enumerate(neighbours(block)):
        columns[pl.ds(start, rows), :, i * chans : (i + 1) * chans] = side


def conv_rows(columns, start, rows, weights):
    width, depth = columns.shape[1:]
    taps = [columns[pl.ds(start + step, rows)].reshape(rows * width, depth) for step in range(3)]
    return jnp.dot(jnp.concatenate(taps, axis=1), weights, preferred_element_type=F32)


def sigmoid(v):
    return 0.5 * jnp.tanh(0.5 * v) + 0.5


def gates_kernel(state_ref, weights_ref, out_ref, columns):
    height, width, chans = state_ref.shape[1:]
    edge_row = jnp.zeros((1,) + columns.shape[1:], BF16)
    columns[0:1] = edge_row
    columns[height + 1 :] = edge_row
    step = 8
    for y in range(0, height, step):
        put_columns(columns, y + 1, state_ref[0, y : y + step].astype(F32))
    weights = weights_ref[...]
    for y in range(0, height, step):
        gates = conv_rows(columns, y, step, weights)
        out_ref[0, y : y + step] = gates.astype(BF16).reshape(step, width, weights.shape[1])


def gates_of(state, weights):
    edges, height, width, chans = state.shape
    outs = weights.shape[1]
    return pl.pallas_call(
        gates_kernel,
        grid=(edges,),
        in_specs=[pl.BlockSpec((1, height, width, chans), lambda e: (e, 0, 0, 0)), whole(weights)],
        out_specs=pl.BlockSpec((1, height, width, outs), lambda e: (e, 0, 0, 0)),
        out_shape=jax.ShapeDtypeStruct((edges, height, width, outs), BF16),
        scratch_shapes=[pltpu.VMEM((height + 2, width, 3 * chans), BF16)],
        compiler_params=pltpu.CompilerParams(vmem_limit_bytes=VMEM_LIMIT),
        cost_estimate=pl.CostEstimate(
            flops=2 * edges * height * width * 9 * chans * outs,
            bytes_accessed=2 * edges * height * width * (chans + outs),
            transcendentals=0,
        ),
        name="gates",
    )(state, weights)


def motion_kernel(low, frames, meta, own, near, *refs):
    fars = refs[:frames]
    flip_ref, mask_ref, base_ref, out_ref, src_buf, raw_buf, tgt_buf, w_buf, sems = refs[frames:]
    step = pl.program_id(0)
    steps = pl.num_programs(0)
    edge = step + low
    height, width, chans = own.shape[2:]
    slot = lax.rem(step, 2)
    lanes = 2 * width
    tiles = base_ref.shape[0]

    def start(e, s):
        def cases(buf, frame):
            far_cases = [((buf == 1) & (frame == f), far) for f, far in enumerate(fars)]
            return [(buf == 0, own.at[frame, 0]), (buf == 2, near.at[frame, 0])] + far_cases

        fetch(cases(meta[e, 0], meta[e, 1]), src_buf.at[s, pl.ds(1, height)], sems.at[0, s])
        fetch(cases(meta[e, 2], meta[e, 3]), raw_buf.at[s], sems.at[1, s])

    @pl.when(step == 0)
    def _():
        start(edge, slot)
        tgt_buf[:, : MARGIN * width] = jnp.zeros((chans, MARGIN * width), BF16)
        below = tgt_buf.shape[1] - (MARGIN + height) * width
        tgt_buf[:, tgt_buf.shape[1] - below :] = jnp.zeros((chans, below), BF16)

    @pl.when(step + 1 < steps)
    def _():
        start(edge + 1, 1 - slot)

    oy, ox = meta[edge, 4], meta[edge, 5]
    for j in range(tiles):
        w_buf[j * lanes : (j + 1) * lanes] = pltpu.roll(base_ref[j], lax.rem(lanes - ox, lanes), 0).astype(BF16)

    await_copy(src_buf.at[slot, pl.ds(1, height)], sems.at[0, slot])
    await_copy(raw_buf.at[slot], sems.at[1, slot])

    flip = flip_ref[...]
    for y in range(0, height, 2):
        block = raw_buf[slot, y : y + 2].reshape(lanes, chans)
        turned = lax.dot_general(block, flip, (((0,), (0,)), ((), ())), preferred_element_type=F32)
        tgt_buf[:, (MARGIN + y) * width : (MARGIN + y + 2) * width] = turned.astype(BF16)

    mask = mask_ref[...]
    keep = mask.astype(BF16)
    odd = lax.rem(oy + 2 * SHIFT, 2)
    weights = w_buf[...]
    unroll = 25

    @pl.loop(0, (height // 2 + unroll) // unroll)
    def _(i):
        starts = [2 * (i * unroll + u) - odd for u in range(unroll)]
        scores = []
        for y in starts:
            lhs = src_buf[slot, pl.ds(y + 1, 2)].reshape(lanes, chans)
            at = (y + oy + SHIFT) // 2 * lanes
            rhs = tgt_buf[:, pl.ds(pl.multiple_of(at, lanes), tiles * lanes)]
            scores.append(jnp.dot(lhs, rhs, preferred_element_type=F32))
        for y, pair in zip(starts, scores):
            volume = []
            for r in range(2):
                parts = []
                for j in range(tiles):
                    tile = pair[r * width : (r + 1) * width, j * lanes : (j + 1) * lanes] * (chans**-0.5)
                    tile = pltpu.roll(tile.astype(BF16), 0, 1, stride=1, stride_axis=0)
                    parts.append(tile * keep)
                volume.append(jnp.concatenate(parts, axis=1))
            res = jnp.dot(jnp.concatenate(volume, axis=0), weights, preferred_element_type=F32)
            out_ref[0, pl.ds(y + 1, 1)] = jnp.maximum(res[:width, :chans], 0.0).astype(BF16)[None]
            out_ref[0, pl.ds(y + 2, 1)] = jnp.maximum(res[width:, chans:], 0.0).astype(BF16)[None]


def motion_constants(width, chans):
    lanes = 2 * width
    rows = SPAN + 1
    place = np.zeros((2, rows // 2, lanes, SPAN * SPAN), np.float32)
    for r in range(rows):
        for b in range(SPAN):
            lane = (width - 1 + RADIUS - b + width * (r % 2)) % lanes
            for parity in range(2):
                if 0 <= r - parity < SPAN:
                    place[parity, r // 2, lane, (r - parity) * SPAN + b] = 1.0
    flip = np.kron(np.eye(2), np.eye(width)[::-1])
    x = np.arange(width)[:, None]
    lane = np.arange(lanes)[None]
    middle = (lane >= width // 2) & (lane < width + width // 2)
    inside = np.where(middle, (lane >= x) & (lane < x + width), np.where(lane < width, x > lane, lane >= x + width))
    return place.astype(BF16), flip.astype(BF16), inside.astype(np.float32)


def motion_weights(w_motion, width):
    place = motion_constants(width, w_motion.shape[1])[0]
    return jnp.concatenate(
        [jnp.einsum("tlk,kc->tlc", side, w_motion, preferred_element_type=F32) for side in place], axis=2
    )


def motion_of(low, high, meta, own, near, fars, base, earlier):
    frames, _, height, width, chans = own.shape
    edges = meta.shape[0]
    rows = SPAN + 1
    _, flip, mask = motion_constants(width, chans)
    buffer_rows = height + 4
    target_rows = height + 2 * MARGIN + 2
    operands = [meta, own, near, *fars, flip, mask, base]
    count = len(operands)
    body = functools.partial(motion_kernel, low, frames)
    if earlier is None:
        kernel, aliases = body, {}
    else:
        kernel, aliases = lambda *refs: body(*refs[:count], *refs[count + 1 :]), {count: 0}
        operands.append(earlier)
    return pl.pallas_call(
        kernel,
        grid_spec=pltpu.PrefetchScalarGridSpec(
            num_scalar_prefetch=1,
            grid=(high - low,),
            in_specs=[any_spec()] * (2 + frames) + [whole(flip), whole(mask), whole(base)] + [any_spec()] * (len(operands) - count),
            out_specs=pl.BlockSpec((1, buffer_rows, width, chans), lambda e, m: (e + low, 0, 0, 0)),
            scratch_shapes=[
                pltpu.VMEM((2, buffer_rows, width, chans), BF16),
                pltpu.VMEM((2, height, width, chans), BF16),
                pltpu.VMEM((chans, target_rows * width), BF16),
                pltpu.VMEM((rows * width, 2 * chans), BF16),
                pltpu.SemaphoreType.DMA((2, 2)),
            ],
        ),
        out_shape=jax.ShapeDtypeStruct((edges, buffer_rows, width, chans), BF16),
        input_output_aliases=aliases,
        compiler_params=pltpu.CompilerParams(vmem_limit_bytes=VMEM_LIMIT),
        cost_estimate=pl.CostEstimate(
            flops=8 * (high - low) * height * width * chans * rows * width,
            bytes_accessed=6 * (high - low) * height * width * chans,
            transcendentals=0,
        ),
        name=f"motion_from{low}",
    )(*operands)


def gru_kernel(
    first,
    last,
    meta,
    own,
    near,
    far_top,
    far_low,
    motion,
    gates,
    state,
    w_input,
    w_candidate,
    _,
    new_ref,
    own_sum,
    far_sum,
    near_top,
    near_low,
    ctx_buf,
    motion_buf,
    gates_buf,
    state_buf,
    columns,
    update_buf,
    drive_buf,
    totals,
    sems,
):
    edge = pl.program_id(0)
    edges = pl.num_programs(0)
    frames = own.shape[0]
    height, width, chans = own.shape[2:]
    slot = edge
    top = max(first - 1, 0)
    end = min(last + 1, height)
    rows = end - top
    split = far_top.shape[1]
    above = min(split - top, rows)
    context_pieces = [
        piece for piece in ((far_top, 0, above, 0), (far_low, above, rows, 4)) if piece[2] > piece[1]
    ]

    def start(e, s):
        buf, frame = meta[e, 0], meta[e, 1]
        pltpu.make_async_copy(motion.at[e, pl.ds(top + 1, rows)], motion_buf.at[s], sems.at[1, s]).start()
        pltpu.make_async_copy(gates.at[e, pl.ds(top, rows)], gates_buf.at[s], sems.at[2, s]).start()
        pltpu.make_async_copy(state.at[e, pl.ds(top, rows)], state_buf.at[s], sems.at[3, s]).start()
        for far, low, high, sem in context_pieces:
            cases = (
                (buf == 0, own.at[frame, 1, pl.ds(top + low, high - low)]),
                (buf == 1, far.at[frame, pl.ds(top + low - (0 if far is far_top else split), high - low)]),
                (buf == 2, near.at[frame, 1, pl.ds(top + low, high - low)]),
            )
            fetch(cases, ctx_buf.at[s, pl.ds(low, high - low)], sems.at[sem, s])

    def finish(s):
        await_copy(motion_buf.at[s], sems.at[1, s])
        await_copy(gates_buf.at[s], sems.at[2, s])
        await_copy(state_buf.at[s], sems.at[3, s])
        for _, low, high, sem in context_pieces:
            await_copy(ctx_buf.at[s, pl.ds(low, high - low)], sems.at[sem, s])

    @pl.when(edge == 0)
    def _():
        for e in range(state.shape[0]):
            start(e, e)
        edge_row = jnp.zeros((1,) + columns.shape[1:], BF16)
        columns[0:1] = edge_row
        columns[rows + 1 :] = edge_row
        totals[...] = jnp.zeros(totals.shape, F32)

    finish(slot)

    weights = w_input[...]
    step = 5
    for y in range(0, rows, step):
        count = min(step, rows - y)
        span = slice(y, y + count)
        mixed = jnp.concatenate([motion_buf[slot, span], ctx_buf[slot, span]], axis=-1)
        inputs = jnp.dot(mixed.reshape(count * width, 2 * chans), weights, preferred_element_type=F32)
        inputs = inputs.reshape(count, width, 3 * chans)
        pre = gates_buf[slot, span].astype(F32)
        update_buf[span] = sigmoid(pre[..., :chans] + inputs[..., :chans])
        reset = sigmoid(pre[..., chans:] + inputs[..., chans : 2 * chans])
        drive_buf[span] = inputs[..., 2 * chans :]
        put_columns(columns, y + 1, reset * state_buf[slot, span].astype(F32))

    weights = w_candidate[...]
    place = meta[edge, 0] * frames + meta[edge, 1]
    step = 12
    for y in range(first, last, step):
        count = min(step, last - y)
        span = slice(y - top, y - top + count)
        conv = conv_rows(columns, y - top, count, weights).reshape(count, width, chans)
        candidate = jnp.tanh(conv + drive_buf[span])
        update = update_buf[span]
        fresh = ((1.0 - update) * state_buf[slot, span].astype(F32) + update * candidate).astype(BF16)
        new_ref[0, y - first : y - first + count] = fresh
        totals[place, y - first : y - first + count] += fresh.astype(F32)

    @pl.when(edge == edges - 1)
    def _():
        half = near_top.shape[1]
        own_sum[...] = totals[:frames].astype(BF16)
        far_sum[...] = totals[frames : 2 * frames].astype(BF16)
        near_top[...] = totals[2 * frames :, :half].astype(BF16)
        near_low[...] = totals[2 * frames :, half:].astype(BF16)


def gru_of(band, meta, own, near, far_top, far_low, motion, gates, state, w_input, w_candidate, earlier):
    frames, _, height, width, chans = own.shape
    edges = state.shape[0]
    size = height // 2
    first, last = band * size, (band + 1) * size
    rows = min(last + 1, height) - max(first - 1, 0)
    sums = jax.ShapeDtypeStruct((frames, size, width, chans), BF16)
    pieces = jax.ShapeDtypeStruct((frames, size // 2, width, chans), BF16)
    sum_spec = pl.BlockSpec(sums.shape, lambda e, m: (0, 0, 0, 0))
    piece_spec = pl.BlockSpec(pieces.shape, lambda e, m: (0, 0, 0, 0))
    body = functools.partial(gru_kernel, first, last)
    operands = [meta, own, near, far_top, far_low, motion, gates, state, w_input, w_candidate]
    if earlier is None:
        kernel = lambda *refs: body(*refs[:10], None, *refs[10:])
        aliases = {}
    else:
        kernel = body
        operands.append(earlier)
        aliases = {10: 0}
    return pl.pallas_call(
        kernel,
        grid_spec=pltpu.PrefetchScalarGridSpec(
            num_scalar_prefetch=1,
            grid=(edges,),
            in_specs=[any_spec()] * 7 + [whole(w_input), whole(w_candidate)] + [any_spec()] * (len(operands) - 10),
            out_specs=[
                pl.BlockSpec((1, size, width, chans), lambda e, m: (e, band, 0, 0)),
                sum_spec,
                sum_spec,
                piece_spec,
                piece_spec,
            ],
            scratch_shapes=[
                pltpu.VMEM((edges, rows, width, chans), BF16),
                pltpu.VMEM((edges, rows, width, chans), BF16),
                pltpu.VMEM((edges, rows, width, 2 * chans), BF16),
                pltpu.VMEM((edges, rows, width, chans), BF16),
                pltpu.VMEM((rows + 2, width, 3 * chans), BF16),
                pltpu.VMEM((rows, width, chans), F32),
                pltpu.VMEM((rows, width, chans), F32),
                pltpu.VMEM((3 * frames, size, width, chans), F32),
                pltpu.SemaphoreType.DMA((5, edges)),
            ],
        ),
        out_shape=[
            jax.ShapeDtypeStruct(state.shape, BF16),
            sums,
            sums,
            pieces,
            pieces,
        ],
        input_output_aliases=aliases,
        compiler_params=pltpu.CompilerParams(vmem_limit_bytes=VMEM_LIMIT),
        cost_estimate=pl.CostEstimate(
            flops=2 * edges * rows * width * chans,
            bytes_accessed=2 * edges * rows * width * chans,
            transcendentals=0,
        ),
        name=f"gru_band{band}",
    )(*operands)


def aggregate_kernel(pieces, first, last, counts, *refs):
    sums, weights_ref, rest = refs[: 4 * len(pieces)], refs[4 * len(pieces)], refs[4 * len(pieces) + 1 :]
    out_ref, columns = rest[-2:]
    width, chans = out_ref.shape[2:]
    edge_row = jnp.zeros((1,) + columns.shape[1:], BF16)
    columns[0:1] = edge_row
    columns[columns.shape[0] - 1 :] = edge_row
    count = counts[pl.program_id(0)]
    at = 1
    for i in range(len(pieces)):
        own, far, *near = sums[4 * i : 4 * i + 4]
        top = 0
        for piece in near[pieces[i][2] :]:
            span = slice(top, top + piece.shape[1])
            total = own[0, span].astype(F32) + far[0, span].astype(F32) + piece[0].astype(F32)
            mean = (total / count).astype(BF16).astype(F32)
            put_columns(columns, at, mean)
            at += piece.shape[1]
            top += piece.shape[1]
    step = 8
    base = 0
    if len(rest) == 3:
        out_ref[0, :first] = rest[0][0]
        base = first
    weights = weights_ref[...]
    skip = 0 if first == 0 else 1
    for y in range(0, last - first, step):
        rows = min(step, last - first - y)
        out = conv_rows(columns, y + skip, rows, weights)
        out_ref[0, base + y : base + y + rows] = out.astype(BF16).reshape(rows, width, chans)


def aggregate_of(first, last, pieces, bands, counts, weights, earlier):
    frames, _, width, chans = bands[0][0].shape
    sums = [array for band in bands for array in band]
    depth = sum(high - low for low, high, _ in pieces)

    def blocks(band, low, high):
        specs = []
        for array in band:
            count = min(high - low, array.shape[1])
            index = low // count if array.shape[1] >= high else array.shape[1] // count - 1 if low else 0
            specs.append(pl.BlockSpec((1, count) + array.shape[2:], lambda f, c, i=index: (f, i, 0, 0)))
        return specs

    rows = last if earlier is not None else last - first
    operands = [counts, *sums, weights]
    more = []
    if earlier is not None:
        operands.append(earlier)
        more = [pl.BlockSpec((1,) + earlier.shape[1:], lambda f, c: (f, 0, 0, 0))]
    return pl.pallas_call(
        functools.partial(aggregate_kernel, pieces, first, last),
        grid_spec=pltpu.PrefetchScalarGridSpec(
            num_scalar_prefetch=1,
            grid=(frames,),
            in_specs=[spec for band, (low, high, _) in zip(bands, pieces) for spec in blocks(band, low, high)]
            + [whole(weights)]
            + more,
            out_specs=pl.BlockSpec((1, rows, width, chans), lambda f, c: (f, 0, 0, 0)),
            scratch_shapes=[pltpu.VMEM((depth + 2, width, 3 * chans), BF16)],
        ),
        out_shape=jax.ShapeDtypeStruct((frames, rows, width, chans), BF16),
        compiler_params=pltpu.CompilerParams(vmem_limit_bytes=16 << 20),
        cost_estimate=pl.CostEstimate(
            flops=2 * frames * (last - first) * width * 9 * chans * chans,
            bytes_accessed=8 * frames * depth * width * chans,
            transcendentals=0,
        ),
        name=f"aggregate_from{first}",
    )(*operands)


def per_device(
    frame_maps, net_state, edges, offsets, w_motion, w_input, w_gates, w_candidate, w_aggregate
):
    frames, _, height, width, chans = frame_maps.shape
    edge_count = net_state.shape[0]
    me = lax.axis_index("rows")
    count = lax.axis_size("rows")
    near_route = [(i, i ^ 1) for i in range(count)]
    far_route = [(i, i + 1 if i % 2 else i - 1) for i in range(1, count - 1)]

    def far_swap(block, *after):
        if after:
            block = lax.optimization_barrier((block,) + after)[0]
        return lax.ppermute(block, "rows", far_route)

    def near_swap(block):
        return lax.ppermute(block, "rows", near_route)

    far_feat, held = [], frame_maps
    for f in range(frames):
        feature = held[f, 0]
        held = lax.optimization_barrier((frame_maps, feature))[0]
        far_feat.append(far_swap(feature))
    near = near_swap(held)

    my_edges = lax.dynamic_slice_in_dim(edges, me * edge_count, edge_count, 0)
    owner = my_edges // frames
    buf = jnp.where(owner == me, 0, jnp.where(owner == (me ^ 1), 2, 1))
    local = my_edges % frames
    meta = jnp.stack(
        [buf[:, 0], local[:, 0], buf[:, 1], local[:, 1], offsets[:, 0], offsets[:, 1]], axis=1
    ).astype(jnp.int32)
    mine = me * frames + jnp.arange(frames, dtype=jnp.int32)
    counts = jnp.maximum(jnp.sum((edges[:, 0][:, None] == mine[None]).astype(F32), axis=0), 1.0)

    base = motion_weights(w_motion, width)
    gates = gates_of(net_state, lax.optimization_barrier((w_gates, near))[0])
    half = 3 * edge_count // 4
    split = height // 2 + 1
    later_maps = lax.optimization_barrier((frame_maps, near))[0]
    context_top, context_low = later_maps[:, 1, :split], later_maps[:, 1, split:]
    held_meta = lax.optimization_barrier((meta, gates, context_top, context_low))[0]
    motion = motion_of(0, half, held_meta, frame_maps, near, far_feat, base, None)
    far_top = far_swap(context_top, motion)
    far_low = far_swap(context_low, motion)
    motion = motion_of(half, edge_count, meta, frame_maps, near, far_feat, base, motion)

    def gru(band, earlier):
        fars = (far_top, far_low if band else far_top)
        return gru_of(band, meta, frame_maps, near, *fars, motion, gates, net_state, w_input, w_candidate, earlier)

    new_state, own_first, far_sum, *near_first = gru(0, None)
    far_first = far_swap(far_sum)
    new_state, own_second, far_sum, *near_second = gru(1, new_state)
    far_second = far_swap(far_sum)
    near_first, near_second = (
        [near_swap(piece) for piece in lax.optimization_barrier((*pieces, far_first))[:2]]
        for pieces in (near_first, near_second)
    )
    first = (own_first, far_first, *near_first)
    second = (own_second, far_second, *near_second)
    size = height // 2
    upper = aggregate_of(0, size - 1, ((0, size, 0),), (first,), counts, w_aggregate, None)
    frame_update = aggregate_of(
        size - 1, height, ((size - 2, size, 1), (0, size, 0)), (first, second), counts, w_aggregate, upper
    )
    return (new_state, frame_update)


def solution(mesh):
    in_specs = (
        P(("groups", "rows"), None, None, None, None),
        P(("groups", "rows"), None, None, None),
        P("groups", None),
        P(("groups", "rows"), None),
        P(),
        P(),
        P(),
        P(),
        P(),
    )
    out_specs = (P(("groups", "rows"), None, None, None), P(("groups", "rows"), None, None, None))
    return jax.shard_map(
        per_device, mesh=mesh, in_specs=in_specs, out_specs=out_specs, check_vma=False
    )
```

```python
import functools

import jax
import jax.numpy as jnp
import numpy as np
from jax import lax
from jax.experimental import pallas as pl
from jax.experimental.pallas import tpu as pltpu
from jax.sharding import PartitionSpec as P

RADIUS = 4
SHIFT = 8
SPAN = 2 * RADIUS + 1
MARGIN = SHIFT + RADIUS
F32 = jnp.float32
BF16 = jnp.bfloat16
VMEM_LIMIT = 60 << 20
MOTION_VMEM_LIMIT = 127 << 19


def any_spec():
    return pl.BlockSpec(memory_space=pl.ANY)


def whole(array):
    return pl.BlockSpec(array.shape, lambda *_: (0,) * array.ndim)


def fetch(cases, dst, sem):
    for condition, src in cases:

        @pl.when(condition)
        def _(src=src):
            pltpu.make_async_copy(src, dst, sem).start()


def await_copy(dst, sem):
    pltpu.make_async_copy(dst, dst, sem).wait()


def neighbours(block):
    rows, width, chans = block.shape
    flat = block.reshape(rows * width, chans)
    x = lax.broadcasted_iota(jnp.int32, (rows, width, chans), 1).reshape(rows * width, chans)
    left = jnp.where(x == 0, 0.0, pltpu.roll(flat, 1, 0)).astype(BF16)
    right = jnp.where(x == width - 1, 0.0, pltpu.roll(flat, rows * width - 1, 0)).astype(BF16)
    return [side.reshape(rows, width, chans) for side in (left, flat.astype(BF16), right)]


def put_columns(columns, start, block):
    chans = block.shape[-1]
    rows = block.shape[0]
    for i, side in enumerate(neighbours(block)):
        columns[pl.ds(start, rows), :, i * chans : (i + 1) * chans] = side


def conv_rows(columns, start, rows, weights):
    width, depth = columns.shape[1:]
    taps = [columns[pl.ds(start + step, rows)].reshape(rows * width, depth) for step in range(3)]
    return jnp.dot(jnp.concatenate(taps, axis=1), weights, preferred_element_type=F32)


def sigmoid(v):
    return 0.5 * jnp.tanh(0.5 * v) + 0.5


def gates_kernel(state_ref, weights_ref, out_ref, columns):
    height, width, chans = state_ref.shape[1:]
    edge_row = jnp.zeros((1,) + columns.shape[1:], BF16)
    columns[0:1] = edge_row
    columns[height + 1 :] = edge_row
    step = 8
    for y in range(0, height, step):
        put_columns(columns, y + 1, state_ref[0, y : y + step].astype(F32))
    weights = weights_ref[...]
    for y in range(0, height, step):
        gates = conv_rows(columns, y, step, weights)
        out_ref[0, y : y + step] = gates.astype(BF16).reshape(step, width, weights.shape[1])


def gates_of(state, weights):
    edges, height, width, chans = state.shape
    outs = weights.shape[1]
    return pl.pallas_call(
        gates_kernel,
        grid=(edges,),
        in_specs=[pl.BlockSpec((1, height, width, chans), lambda e: (e, 0, 0, 0)), whole(weights)],
        out_specs=pl.BlockSpec((1, height, width, outs), lambda e: (e, 0, 0, 0)),
        out_shape=jax.ShapeDtypeStruct((edges, height, width, outs), BF16),
        scratch_shapes=[pltpu.VMEM((height + 2, width, 3 * chans), BF16)],
        compiler_params=pltpu.CompilerParams(vmem_limit_bytes=VMEM_LIMIT),
        cost_estimate=pl.CostEstimate(
            flops=2 * edges * height * width * 9 * chans * outs,
            bytes_accessed=2 * edges * height * width * (chans + outs),
            transcendentals=0,
        ),
        name="gates",
    )(state, weights)


def motion_kernel(low, meta, own, near, far, flip_ref, mask_ref, base_ref, out_ref, src_buf, raw_buf, tgt_buf, w_buf, sems):
    step = pl.program_id(0)
    steps = pl.num_programs(0)
    edge = step + low
    height, width, chans = own.shape[2:]
    slot = lax.rem(step, 2)
    lanes = 2 * width
    tiles = base_ref.shape[0]

    def start(e, s):
        def cases(buf, frame):
            return ((buf == 0, own.at[frame, 0]), (buf == 1, far.at[frame]), (buf == 2, near.at[frame, 0]))

        fetch(cases(meta[e, 0], meta[e, 1]), src_buf.at[s, pl.ds(1, height)], sems.at[0, s])
        fetch(cases(meta[e, 2], meta[e, 3]), raw_buf.at[s], sems.at[1, s])

    @pl.when(step == 0)
    def _():
        start(edge, slot)
        tgt_buf[:, : MARGIN * width] = jnp.zeros((chans, MARGIN * width), BF16)
        below = tgt_buf.shape[1] - (MARGIN + height) * width
        tgt_buf[:, tgt_buf.shape[1] - below :] = jnp.zeros((chans, below), BF16)

    @pl.when(step + 1 < steps)
    def _():
        start(edge + 1, 1 - slot)

    oy, ox = meta[edge, 4], meta[edge, 5]
    for j in range(tiles):
        w_buf[j * lanes : (j + 1) * lanes] = pltpu.roll(base_ref[j], lax.rem(lanes - ox, lanes), 0).astype(BF16)

    await_copy(src_buf.at[slot, pl.ds(1, height)], sems.at[0, slot])
    await_copy(raw_buf.at[slot], sems.at[1, slot])

    flip = flip_ref[...]
    for y in range(0, height, 2):
        block = raw_buf[slot, y : y + 2].reshape(lanes, chans)
        turned = lax.dot_general(block, flip, (((0,), (0,)), ((), ())), preferred_element_type=F32)
        tgt_buf[:, (MARGIN + y) * width : (MARGIN + y + 2) * width] = turned.astype(BF16)

    mask = mask_ref[...]
    keep = mask.astype(BF16)
    odd = lax.rem(oy + 2 * SHIFT, 2)
    weights = w_buf[...]
    unroll = 25

    @pl.loop(0, (height // 2 + unroll) // unroll)
    def _(i):
        starts = [2 * (i * unroll + u) - odd for u in range(unroll)]
        scores = []
        for y in starts:
            lhs = src_buf[slot, pl.ds(y + 1, 2)].reshape(lanes, chans)
            at = (y + oy + SHIFT) // 2 * lanes
            rhs = tgt_buf[:, pl.ds(pl.multiple_of(at, lanes), tiles * lanes)]
            scores.append(jnp.dot(lhs, rhs, preferred_element_type=F32))
        for y, pair in zip(starts, scores):
            volume = []
            for r in range(2):
                parts = []
                for j in range(tiles):
                    tile = pair[r * width : (r + 1) * width, j * lanes : (j + 1) * lanes] * (chans**-0.5)
                    tile = pltpu.roll(tile.astype(BF16), 0, 1, stride=1, stride_axis=0)
                    parts.append(tile * keep)
                volume.append(jnp.concatenate(parts, axis=1))
            res = jnp.dot(jnp.concatenate(volume, axis=0), weights, preferred_element_type=F32)
            out_ref[0, pl.ds(y + 1, 1)] = jnp.maximum(res[:width, :chans], 0.0).astype(BF16)[None]
            out_ref[0, pl.ds(y + 2, 1)] = jnp.maximum(res[width:, chans:], 0.0).astype(BF16)[None]


def motion_constants(width, chans):
    lanes = 2 * width
    rows = SPAN + 1
    place = np.zeros((2, rows // 2, lanes, SPAN * SPAN), np.float32)
    for r in range(rows):
        for b in range(SPAN):
            lane = (width - 1 + RADIUS - b + width * (r % 2)) % lanes
            for parity in range(2):
                if 0 <= r - parity < SPAN:
                    place[parity, r // 2, lane, (r - parity) * SPAN + b] = 1.0
    flip = np.kron(np.eye(2), np.eye(width)[::-1])
    x = np.arange(width)[:, None]
    lane = np.arange(lanes)[None]
    middle = (lane >= width // 2) & (lane < width + width // 2)
    inside = np.where(middle, (lane >= x) & (lane < x + width), np.where(lane < width, x > lane, lane >= x + width))
    return place.astype(BF16), flip.astype(BF16), inside.astype(np.float32)


def motion_weights(w_motion, width):
    place = motion_constants(width, w_motion.shape[1])[0]
    return jnp.concatenate(
        [jnp.einsum("tlk,kc->tlc", side, w_motion, preferred_element_type=F32) for side in place], axis=2
    )


def motion_of(low, high, meta, own, near, far, base, earlier):
    _, _, height, width, chans = own.shape
    edges = meta.shape[0]
    rows = SPAN + 1
    _, flip, mask = motion_constants(width, chans)
    buffer_rows = height + 4
    target_rows = height + 2 * MARGIN + 2
    operands = [meta, own, near, far, flip, mask, base]
    count = len(operands)
    body = functools.partial(motion_kernel, low)
    if earlier is None:
        kernel, aliases = body, {}
    else:
        kernel, aliases = lambda *refs: body(*refs[:count], *refs[count + 1 :]), {count: 0}
        operands.append(earlier)
    return pl.pallas_call(
        kernel,
        grid_spec=pltpu.PrefetchScalarGridSpec(
            num_scalar_prefetch=1,
            grid=(high - low,),
            in_specs=[any_spec()] * 3 + [whole(flip), whole(mask), whole(base)] + [any_spec()] * (len(operands) - count),
            out_specs=pl.BlockSpec((1, buffer_rows, width, chans), lambda e, m: (e + low, 0, 0, 0)),
            scratch_shapes=[
                pltpu.VMEM((2, buffer_rows, width, chans), BF16),
                pltpu.VMEM((2, height, width, chans), BF16),
                pltpu.VMEM((chans, target_rows * width), BF16),
                pltpu.VMEM((rows * width, 2 * chans), BF16),
                pltpu.SemaphoreType.DMA((2, 2)),
            ],
        ),
        out_shape=jax.ShapeDtypeStruct((edges, buffer_rows, width, chans), BF16),
        input_output_aliases=aliases,
        compiler_params=pltpu.CompilerParams(vmem_limit_bytes=MOTION_VMEM_LIMIT),
        cost_estimate=pl.CostEstimate(
            flops=8 * (high - low) * height * width * chans * rows * width,
            bytes_accessed=6 * (high - low) * height * width * chans,
            transcendentals=0,
        ),
        name=f"motion_from{low}",
    )(*operands)


def gru_kernel(
    first,
    last,
    meta,
    own,
    near,
    far_top,
    far_low,
    motion,
    gates,
    state,
    w_input,
    w_candidate,
    _,
    new_ref,
    own_sum,
    far_sum,
    near_top,
    near_low,
    ctx_buf,
    motion_buf,
    gates_buf,
    state_buf,
    columns,
    update_buf,
    drive_buf,
    totals,
    sems,
):
    edge = pl.program_id(0)
    edges = pl.num_programs(0)
    frames = own.shape[0]
    height, width, chans = own.shape[2:]
    slot = edge
    top = max(first - 1, 0)
    end = min(last + 1, height)
    rows = end - top
    split = far_top.shape[1]
    above = min(split - top, rows)
    context_pieces = [
        piece for piece in ((far_top, 0, above, 0), (far_low, above, rows, 4)) if piece[2] > piece[1]
    ]

    def start(e, s):
        buf, frame = meta[e, 0], meta[e, 1]
        pltpu.make_async_copy(motion.at[e, pl.ds(top + 1, rows)], motion_buf.at[s], sems.at[1, s]).start()
        pltpu.make_async_copy(gates.at[e, pl.ds(top, rows)], gates_buf.at[s], sems.at[2, s]).start()
        pltpu.make_async_copy(state.at[e, pl.ds(top, rows)], state_buf.at[s], sems.at[3, s]).start()
        for far, low, high, sem in context_pieces:
            cases = (
                (buf == 0, own.at[frame, 1, pl.ds(top + low, high - low)]),
                (buf == 1, far.at[frame, pl.ds(top + low - (0 if far is far_top else split), high - low)]),
                (buf == 2, near.at[frame, 1, pl.ds(top + low, high - low)]),
            )
            fetch(cases, ctx_buf.at[s, pl.ds(low, high - low)], sems.at[sem, s])

    def finish(s):
        await_copy(motion_buf.at[s], sems.at[1, s])
        await_copy(gates_buf.at[s], sems.at[2, s])
        await_copy(state_buf.at[s], sems.at[3, s])
        for _, low, high, sem in context_pieces:
            await_copy(ctx_buf.at[s, pl.ds(low, high - low)], sems.at[sem, s])

    @pl.when(edge == 0)
    def _():
        for e in range(state.shape[0]):
            start(e, e)
        edge_row = jnp.zeros((1,) + columns.shape[1:], BF16)
        columns[0:1] = edge_row
        columns[rows + 1 :] = edge_row
        totals[...] = jnp.zeros(totals.shape, F32)

    finish(slot)

    weights = w_input[...]
    step = 5
    for y in range(0, rows, step):
        count = min(step, rows - y)
        span = slice(y, y + count)
        mixed = jnp.concatenate([motion_buf[slot, span], ctx_buf[slot, span]], axis=-1)
        inputs = jnp.dot(mixed.reshape(count * width, 2 * chans), weights, preferred_element_type=F32)
        inputs = inputs.reshape(count, width, 3 * chans)
        pre = gates_buf[slot, span].astype(F32)
        update_buf[span] = sigmoid(pre[..., :chans] + inputs[..., :chans])
        reset = sigmoid(pre[..., chans:] + inputs[..., chans : 2 * chans])
        drive_buf[span] = inputs[..., 2 * chans :]
        put_columns(columns, y + 1, reset * state_buf[slot, span].astype(F32))

    weights = w_candidate[...]
    place = meta[edge, 0] * frames + meta[edge, 1]
    step = 12
    for y in range(first, last, step):
        count = min(step, last - y)
        span = slice(y - top, y - top + count)
        conv = conv_rows(columns, y - top, count, weights).reshape(count, width, chans)
        candidate = jnp.tanh(conv + drive_buf[span])
        update = update_buf[span]
        fresh = ((1.0 - update) * state_buf[slot, span].astype(F32) + update * candidate).astype(BF16)
        new_ref[0, y - first : y - first + count] = fresh
        totals[place, y - first : y - first + count] += fresh.astype(F32)

    @pl.when(edge == edges - 1)
    def _():
        half = near_top.shape[1]
        own_sum[...] = totals[:frames].astype(BF16)
        far_sum[...] = totals[frames : 2 * frames].astype(BF16)
        near_top[...] = totals[2 * frames :, :half].astype(BF16)
        near_low[...] = totals[2 * frames :, half:].astype(BF16)


def gru_of(band, meta, own, near, far_top, far_low, motion, gates, state, w_input, w_candidate, earlier):
    frames, _, height, width, chans = own.shape
    edges = state.shape[0]
    size = height // 2
    first, last = band * size, (band + 1) * size
    rows = min(last + 1, height) - max(first - 1, 0)
    sums = jax.ShapeDtypeStruct((frames, size, width, chans), BF16)
    pieces = jax.ShapeDtypeStruct((frames, size // 2, width, chans), BF16)
    sum_spec = pl.BlockSpec(sums.shape, lambda e, m: (0, 0, 0, 0))
    piece_spec = pl.BlockSpec(pieces.shape, lambda e, m: (0, 0, 0, 0))
    body = functools.partial(gru_kernel, first, last)
    operands = [meta, own, near, far_top, far_low, motion, gates, state, w_input, w_candidate]
    if earlier is None:
        kernel = lambda *refs: body(*refs[:10], None, *refs[10:])
        aliases = {}
    else:
        kernel = body
        operands.append(earlier)
        aliases = {10: 0}
    return pl.pallas_call(
        kernel,
        grid_spec=pltpu.PrefetchScalarGridSpec(
            num_scalar_prefetch=1,
            grid=(edges,),
            in_specs=[any_spec()] * 7 + [whole(w_input), whole(w_candidate)] + [any_spec()] * (len(operands) - 10),
            out_specs=[
                pl.BlockSpec((1, size, width, chans), lambda e, m: (e, band, 0, 0)),
                sum_spec,
                sum_spec,
                piece_spec,
                piece_spec,
            ],
            scratch_shapes=[
                pltpu.VMEM((edges, rows, width, chans), BF16),
                pltpu.VMEM((edges, rows, width, chans), BF16),
                pltpu.VMEM((edges, rows, width, 2 * chans), BF16),
                pltpu.VMEM((edges, rows, width, chans), BF16),
                pltpu.VMEM((rows + 2, width, 3 * chans), BF16),
                pltpu.VMEM((rows, width, chans), F32),
                pltpu.VMEM((rows, width, chans), F32),
                pltpu.VMEM((3 * frames, size, width, chans), F32),
                pltpu.SemaphoreType.DMA((5, edges)),
            ],
        ),
        out_shape=[
            jax.ShapeDtypeStruct(state.shape, BF16),
            sums,
            sums,
            pieces,
            pieces,
        ],
        input_output_aliases=aliases,
        compiler_params=pltpu.CompilerParams(vmem_limit_bytes=VMEM_LIMIT),
        cost_estimate=pl.CostEstimate(
            flops=2 * edges * rows * width * chans,
            bytes_accessed=2 * edges * rows * width * chans,
            transcendentals=0,
        ),
        name=f"gru_band{band}",
    )(*operands)


def aggregate_kernel(pieces, first, last, counts, *refs):
    sums, weights_ref, rest = refs[: 4 * len(pieces)], refs[4 * len(pieces)], refs[4 * len(pieces) + 1 :]
    out_ref, columns = rest[-2:]
    width, chans = out_ref.shape[2:]
    edge_row = jnp.zeros((1,) + columns.shape[1:], BF16)
    columns[0:1] = edge_row
    columns[columns.shape[0] - 1 :] = edge_row
    count = counts[pl.program_id(0)]
    at = 1
    for i in range(len(pieces)):
        own, far, *near = sums[4 * i : 4 * i + 4]
        top = 0
        for piece in near[pieces[i][2] :]:
            span = slice(top, top + piece.shape[1])
            total = own[0, span].astype(F32) + far[0, span].astype(F32) + piece[0].astype(F32)
            mean = (total / count).astype(BF16).astype(F32)
            put_columns(columns, at, mean)
            at += piece.shape[1]
            top += piece.shape[1]
    step = 8
    base = 0
    if len(rest) == 3:
        out_ref[0, :first] = rest[0][0]
        base = first
    weights = weights_ref[...]
    skip = 0 if first == 0 else 1
    for y in range(0, last - first, step):
        rows = min(step, last - first - y)
        out = conv_rows(columns, y + skip, rows, weights)
        out_ref[0, base + y : base + y + rows] = out.astype(BF16).reshape(rows, width, chans)


def aggregate_of(first, last, pieces, bands, counts, weights, earlier):
    frames, _, width, chans = bands[0][0].shape
    sums = [array for band in bands for array in band]
    depth = sum(high - low for low, high, _ in pieces)

    def blocks(band, low, high):
        specs = []
        for array in band:
            count = min(high - low, array.shape[1])
            index = low // count if array.shape[1] >= high else array.shape[1] // count - 1 if low else 0
            specs.append(pl.BlockSpec((1, count) + array.shape[2:], lambda f, c, i=index: (f, i, 0, 0)))
        return specs

    rows = last if earlier is not None else last - first
    operands = [counts, *sums, weights]
    more = []
    if earlier is not None:
        operands.append(earlier)
        more = [pl.BlockSpec((1,) + earlier.shape[1:], lambda f, c: (f, 0, 0, 0))]
    return pl.pallas_call(
        functools.partial(aggregate_kernel, pieces, first, last),
        grid_spec=pltpu.PrefetchScalarGridSpec(
            num_scalar_prefetch=1,
            grid=(frames,),
            in_specs=[spec for band, (low, high, _) in zip(bands, pieces) for spec in blocks(band, low, high)]
            + [whole(weights)]
            + more,
            out_specs=pl.BlockSpec((1, rows, width, chans), lambda f, c: (f, 0, 0, 0)),
            scratch_shapes=[pltpu.VMEM((depth + 2, width, 3 * chans), BF16)],
        ),
        out_shape=jax.ShapeDtypeStruct((frames, rows, width, chans), BF16),
        compiler_params=pltpu.CompilerParams(vmem_limit_bytes=16 << 20),
        cost_estimate=pl.CostEstimate(
            flops=2 * frames * (last - first) * width * 9 * chans * chans,
            bytes_accessed=8 * frames * depth * width * chans,
            transcendentals=0,
        ),
        name=f"aggregate_from{first}",
    )(*operands)


def per_device(
    frame_maps, net_state, edges, offsets, w_motion, w_input, w_gates, w_candidate, w_aggregate
):
    frames, _, height, width, chans = frame_maps.shape
    edge_count = net_state.shape[0]
    me = lax.axis_index("rows")
    count = lax.axis_size("rows")
    near_route = [(i, i ^ 1) for i in range(count)]
    far_route = [(i, i + 1 if i % 2 else i - 1) for i in range(1, count - 1)]

    def far_swap(block, *after):
        if after:
            block = lax.optimization_barrier((block,) + after)[0]
        return lax.ppermute(block, "rows", far_route)

    def near_swap(block):
        return lax.ppermute(block, "rows", near_route)

    features = frame_maps[:, 0]
    far_feat = far_swap(features)
    near = near_swap(lax.optimization_barrier((frame_maps, features))[0])

    my_edges = lax.dynamic_slice_in_dim(edges, me * edge_count, edge_count, 0)
    owner = my_edges // frames
    buf = jnp.where(owner == me, 0, jnp.where(owner == (me ^ 1), 2, 1))
    local = my_edges % frames
    meta = jnp.stack(
        [buf[:, 0], local[:, 0], buf[:, 1], local[:, 1], offsets[:, 0], offsets[:, 1]], axis=1
    ).astype(jnp.int32)
    mine = me * frames + jnp.arange(frames, dtype=jnp.int32)
    counts = jnp.maximum(jnp.sum((edges[:, 0][:, None] == mine[None]).astype(F32), axis=0), 1.0)

    base = motion_weights(w_motion, width)
    gates = gates_of(net_state, lax.optimization_barrier((w_gates, near))[0])
    half = 3 * edge_count // 4
    split = height // 2 + 1
    later_maps = lax.optimization_barrier((frame_maps, near))[0]
    context_top, context_low = later_maps[:, 1, :split], later_maps[:, 1, split:]
    held_meta = lax.optimization_barrier((meta, gates, context_top, context_low))[0]
    motion = motion_of(0, half, held_meta, frame_maps, near, far_feat, base, None)
    far_top = far_swap(context_top, motion)
    far_low = far_swap(context_low, motion)
    motion = motion_of(half, edge_count, meta, frame_maps, near, far_feat, base, motion)

    def gru(band, earlier):
        fars = (far_top, far_low if band else far_top)
        return gru_of(band, meta, frame_maps, near, *fars, motion, gates, net_state, w_input, w_candidate, earlier)

    new_state, own_first, far_sum, *near_first = gru(0, None)
    far_first = far_swap(far_sum)
    new_state, own_second, far_sum, *near_second = gru(1, new_state)
    far_second = far_swap(far_sum)
    near_first, near_second = (
        [near_swap(piece) for piece in lax.optimization_barrier((*pieces, far_first))[:2]]
        for pieces in (near_first, near_second)
    )
    first = (own_first, far_first, *near_first)
    second = (own_second, far_second, *near_second)
    size = height // 2
    upper = aggregate_of(0, size - 1, ((0, size, 0),), (first,), counts, w_aggregate, None)
    frame_update = aggregate_of(
        size - 1, height, ((size - 2, size, 1), (0, size, 0)), (first, second), counts, w_aggregate, upper
    )
    return (new_state, frame_update)


def solution(mesh):
    in_specs = (
        P(("groups", "rows"), None, None, None, None),
        P(("groups", "rows"), None, None, None),
        P("groups", None),
        P(("groups", "rows"), None),
        P(),
        P(),
        P(),
        P(),
        P(),
    )
    out_specs = (P(("groups", "rows"), None, None, None), P(("groups", "rows"), None, None, None))
    return jax.shard_map(
        per_device, mesh=mesh, in_specs=in_specs, out_specs=out_specs, check_vma=False
    )
```

```python
import functools

import jax
import jax.numpy as jnp
import numpy as np
from jax import lax
from jax.experimental import pallas as pl
from jax.experimental.pallas import tpu as pltpu
from jax.sharding import PartitionSpec as P

RADIUS = 4
SHIFT = 8
SPAN = 2 * RADIUS + 1
MARGIN = SHIFT + RADIUS
F32 = jnp.float32
BF16 = jnp.bfloat16
VMEM_LIMIT = 60 << 20
MOTION_VMEM_LIMIT = 127 << 19


def any_spec():
    return pl.BlockSpec(memory_space=pl.ANY)


def whole(array):
    return pl.BlockSpec(array.shape, lambda *_: (0,) * array.ndim)


def fetch(cases, dst, sem):
    for condition, src in cases:

        @pl.when(condition)
        def _(src=src):
            pltpu.make_async_copy(src, dst, sem).start()


def await_copy(dst, sem):
    pltpu.make_async_copy(dst, dst, sem).wait()


def neighbours(block):
    rows, width, chans = block.shape
    flat = block.reshape(rows * width, chans)
    x = lax.broadcasted_iota(jnp.int32, (rows, width, chans), 1).reshape(rows * width, chans)
    left = jnp.where(x == 0, 0.0, pltpu.roll(flat, 1, 0)).astype(BF16)
    right = jnp.where(x == width - 1, 0.0, pltpu.roll(flat, rows * width - 1, 0)).astype(BF16)
    return [side.reshape(rows, width, chans) for side in (left, flat.astype(BF16), right)]


def put_columns(columns, start, block):
    chans = block.shape[-1]
    rows = block.shape[0]
    for i, side in enumerate(neighbours(block)):
        columns[pl.ds(start, rows), :, i * chans : (i + 1) * chans] = side


def conv_rows(columns, start, rows, weights):
    width, depth = columns.shape[1:]
    taps = [columns[pl.ds(start + step, rows)].reshape(rows * width, depth) for step in range(3)]
    return jnp.dot(jnp.concatenate(taps, axis=1), weights, preferred_element_type=F32)


def sigmoid(v):
    return 0.5 * jnp.tanh(0.5 * v) + 0.5


def gates_kernel(state_ref, weights_ref, out_ref, columns):
    height, width, chans = state_ref.shape[1:]
    edge_row = jnp.zeros((1,) + columns.shape[1:], BF16)
    columns[0:1] = edge_row
    columns[height + 1 :] = edge_row
    step = 8
    for y in range(0, height, step):
        put_columns(columns, y + 1, state_ref[0, y : y + step].astype(F32))
    weights = weights_ref[...]
    for y in range(0, height, step):
        gates = conv_rows(columns, y, step, weights)
        out_ref[0, y : y + step] = gates.astype(BF16).reshape(step, width, weights.shape[1])


def gates_of(state, weights):
    edges, height, width, chans = state.shape
    outs = weights.shape[1]
    return pl.pallas_call(
        gates_kernel,
        grid=(edges,),
        in_specs=[pl.BlockSpec((1, height, width, chans), lambda e: (e, 0, 0, 0)), whole(weights)],
        out_specs=pl.BlockSpec((1, height, width, outs), lambda e: (e, 0, 0, 0)),
        out_shape=jax.ShapeDtypeStruct((edges, height, width, outs), BF16),
        scratch_shapes=[pltpu.VMEM((height + 2, width, 3 * chans), BF16)],
        compiler_params=pltpu.CompilerParams(vmem_limit_bytes=VMEM_LIMIT),
        cost_estimate=pl.CostEstimate(
            flops=2 * edges * height * width * 9 * chans * outs,
            bytes_accessed=2 * edges * height * width * (chans + outs),
            transcendentals=0,
        ),
        name="gates",
    )(state, weights)


def motion_kernel(low, meta, own, near, far, flip_ref, mask_ref, base_ref, out_ref, src_buf, raw_buf, tgt_buf, w_buf, sems):
    step = pl.program_id(0)
    steps = pl.num_programs(0)
    edge = step + low
    height, width, chans = own.shape[2:]
    slot = lax.rem(step, 2)
    lanes = 2 * width
    tiles = base_ref.shape[0]

    def start(e, s):
        def cases(buf, frame):
            return ((buf == 0, own.at[frame, 0]), (buf == 1, far.at[frame]), (buf == 2, near.at[frame, 0]))

        fetch(cases(meta[e, 0], meta[e, 1]), src_buf.at[s, pl.ds(1, height)], sems.at[0, s])
        fetch(cases(meta[e, 2], meta[e, 3]), raw_buf.at[s], sems.at[1, s])

    @pl.when(step == 0)
    def _():
        start(edge, slot)
        tgt_buf[:, : MARGIN * width] = jnp.zeros((chans, MARGIN * width), BF16)
        below = tgt_buf.shape[1] - (MARGIN + height) * width
        tgt_buf[:, tgt_buf.shape[1] - below :] = jnp.zeros((chans, below), BF16)

    @pl.when(step + 1 < steps)
    def _():
        start(edge + 1, 1 - slot)

    oy, ox = meta[edge, 4], meta[edge, 5]
    for j in range(tiles):
        w_buf[j * lanes : (j + 1) * lanes] = pltpu.roll(base_ref[j], lax.rem(lanes - ox, lanes), 0).astype(BF16)

    await_copy(src_buf.at[slot, pl.ds(1, height)], sems.at[0, slot])
    await_copy(raw_buf.at[slot], sems.at[1, slot])

    flip = flip_ref[...]
    for y in range(0, height, 2):
        block = raw_buf[slot, y : y + 2].reshape(lanes, chans)
        turned = lax.dot_general(block, flip, (((0,), (0,)), ((), ())), preferred_element_type=F32)
        tgt_buf[:, (MARGIN + y) * width : (MARGIN + y + 2) * width] = turned.astype(BF16)

    mask = mask_ref[...]
    keep = mask.astype(BF16)
    odd = lax.rem(oy + 2 * SHIFT, 2)
    weights = w_buf[...]
    unroll = 25

    @pl.loop(0, (height // 2 + unroll) // unroll)
    def _(i):
        starts = [2 * (i * unroll + u) - odd for u in range(unroll)]
        scores = []
        for y in starts:
            lhs = src_buf[slot, pl.ds(y + 1, 2)].reshape(lanes, chans)
            at = (y + oy + SHIFT) // 2 * lanes
            rhs = tgt_buf[:, pl.ds(pl.multiple_of(at, lanes), tiles * lanes)]
            scores.append(jnp.dot(lhs, rhs, preferred_element_type=F32))
        for y, pair in zip(starts, scores):
            volume = []
            for r in range(2):
                parts = []
                for j in range(tiles):
                    tile = pair[r * width : (r + 1) * width, j * lanes : (j + 1) * lanes] * (chans**-0.5)
                    tile = pltpu.roll(tile.astype(BF16), 0, 1, stride=1, stride_axis=0)
                    parts.append(tile * keep)
                volume.append(jnp.concatenate(parts, axis=1))
            res = jnp.dot(jnp.concatenate(volume, axis=0), weights, preferred_element_type=F32)
            out_ref[0, pl.ds(y + 1, 1)] = jnp.maximum(res[:width, :chans], 0.0).astype(BF16)[None]
            out_ref[0, pl.ds(y + 2, 1)] = jnp.maximum(res[width:, chans:], 0.0).astype(BF16)[None]


def motion_constants(width, chans):
    lanes = 2 * width
    rows = SPAN + 1
    place = np.zeros((2, rows // 2, lanes, SPAN * SPAN), np.float32)
    for r in range(rows):
        for b in range(SPAN):
            lane = (width - 1 + RADIUS - b + width * (r % 2)) % lanes
            for parity in range(2):
                if 0 <= r - parity < SPAN:
                    place[parity, r // 2, lane, (r - parity) * SPAN + b] = 1.0
    flip = np.kron(np.eye(2), np.eye(width)[::-1])
    x = np.arange(width)[:, None]
    lane = np.arange(lanes)[None]
    middle = (lane >= width // 2) & (lane < width + width // 2)
    inside = np.where(middle, (lane >= x) & (lane < x + width), np.where(lane < width, x > lane, lane >= x + width))
    return place.astype(BF16), flip.astype(BF16), inside.astype(np.float32)


def motion_weights(w_motion, width):
    place = motion_constants(width, w_motion.shape[1])[0]
    return jnp.concatenate(
        [jnp.einsum("tlk,kc->tlc", side, w_motion, preferred_element_type=F32) for side in place], axis=2
    )


def motion_of(low, high, meta, own, near, far, base, earlier):
    _, _, height, width, chans = own.shape
    edges = meta.shape[0]
    rows = SPAN + 1
    _, flip, mask = motion_constants(width, chans)
    buffer_rows = height + 4
    target_rows = height + 2 * MARGIN + 2
    operands = [meta, own, near, far, flip, mask, base]
    count = len(operands)
    body = functools.partial(motion_kernel, low)
    if earlier is None:
        kernel, aliases = body, {}
    else:
        kernel, aliases = lambda *refs: body(*refs[:count], *refs[count + 1 :]), {count: 0}
        operands.append(earlier)
    return pl.pallas_call(
        kernel,
        grid_spec=pltpu.PrefetchScalarGridSpec(
            num_scalar_prefetch=1,
            grid=(high - low,),
            in_specs=[any_spec()] * 3 + [whole(flip), whole(mask), whole(base)] + [any_spec()] * (len(operands) - count),
            out_specs=pl.BlockSpec((1, buffer_rows, width, chans), lambda e, m: (e + low, 0, 0, 0)),
            scratch_shapes=[
                pltpu.VMEM((2, buffer_rows, width, chans), BF16),
                pltpu.VMEM((2, height, width, chans), BF16),
                pltpu.VMEM((chans, target_rows * width), BF16),
                pltpu.VMEM((rows * width, 2 * chans), BF16),
                pltpu.SemaphoreType.DMA((2, 2)),
            ],
        ),
        out_shape=jax.ShapeDtypeStruct((edges, buffer_rows, width, chans), BF16),
        input_output_aliases=aliases,
        compiler_params=pltpu.CompilerParams(vmem_limit_bytes=MOTION_VMEM_LIMIT),
        cost_estimate=pl.CostEstimate(
            flops=8 * (high - low) * height * width * chans * rows * width,
            bytes_accessed=6 * (high - low) * height * width * chans,
            transcendentals=0,
        ),
        name=f"motion_from{low}",
    )(*operands)


def gru_kernel(
    first,
    last,
    meta,
    own,
    near,
    far_top,
    far_low,
    motion,
    gates,
    state,
    w_input,
    w_candidate,
    _,
    new_ref,
    own_sum,
    far_sum,
    near_top,
    near_low,
    ctx_buf,
    motion_buf,
    gates_buf,
    state_buf,
    columns,
    update_buf,
    drive_buf,
    totals,
    sems,
):
    edge = pl.program_id(0)
    edges = pl.num_programs(0)
    frames = own.shape[0]
    height, width, chans = own.shape[2:]
    slot = lax.rem(edge, 2)
    top = max(first - 1, 0)
    end = min(last + 1, height)
    rows = end - top
    split = far_top.shape[1]
    above = min(split - top, rows)
    context_pieces = [
        piece for piece in ((far_top, 0, above, 0), (far_low, above, rows, 4)) if piece[2] > piece[1]
    ]

    def start(e, s):
        buf, frame = meta[e, 0], meta[e, 1]
        pltpu.make_async_copy(motion.at[e, pl.ds(top + 1, rows)], motion_buf.at[s], sems.at[1, s]).start()
        pltpu.make_async_copy(gates.at[e, pl.ds(top, rows)], gates_buf.at[s], sems.at[2, s]).start()
        pltpu.make_async_copy(state.at[e, pl.ds(top, rows)], state_buf.at[s], sems.at[3, s]).start()
        for far, low, high, sem in context_pieces:
            cases = (
                (buf == 0, own.at[frame, 1, pl.ds(top + low, high - low)]),
                (buf == 1, far.at[frame, pl.ds(top + low - (0 if far is far_top else split), high - low)]),
                (buf == 2, near.at[frame, 1, pl.ds(top + low, high - low)]),
            )
            fetch(cases, ctx_buf.at[s, pl.ds(low, high - low)], sems.at[sem, s])

    def finish(s):
        await_copy(motion_buf.at[s], sems.at[1, s])
        await_copy(gates_buf.at[s], sems.at[2, s])
        await_copy(state_buf.at[s], sems.at[3, s])
        for _, low, high, sem in context_pieces:
            await_copy(ctx_buf.at[s, pl.ds(low, high - low)], sems.at[sem, s])

    @pl.when(edge == 0)
    def _():
        start(edge, slot)
        edge_row = jnp.zeros((1,) + columns.shape[1:], BF16)
        columns[0:1] = edge_row
        columns[rows + 1 :] = edge_row
        totals[...] = jnp.zeros(totals.shape, F32)

    @pl.when(edge + 1 < edges)
    def _():
        start(edge + 1, 1 - slot)

    finish(slot)

    weights = w_input[...]
    step = 5
    for y in range(0, rows, step):
        count = min(step, rows - y)
        span = slice(y, y + count)
        mixed = jnp.concatenate([motion_buf[slot, span], ctx_buf[slot, span]], axis=-1)
        inputs = jnp.dot(mixed.reshape(count * width, 2 * chans), weights, preferred_element_type=F32)
        inputs = inputs.reshape(count, width, 3 * chans)
        pre = gates_buf[slot, span].astype(F32)
        update_buf[span] = sigmoid(pre[..., :chans] + inputs[..., :chans])
        reset = sigmoid(pre[..., chans:] + inputs[..., chans : 2 * chans])
        drive_buf[span] = inputs[..., 2 * chans :]
        put_columns(columns, y + 1, reset * state_buf[slot, span].astype(F32))

    weights = w_candidate[...]
    place = meta[edge, 0] * frames + meta[edge, 1]
    step = 12
    for y in range(first, last, step):
        count = min(step, last - y)
        span = slice(y - top, y - top + count)
        conv = conv_rows(columns, y - top, count, weights).reshape(count, width, chans)
        candidate = jnp.tanh(conv + drive_buf[span])
        update = update_buf[span]
        fresh = ((1.0 - update) * state_buf[slot, span].astype(F32) + update * candidate).astype(BF16)
        new_ref[0, y - first : y - first + count] = fresh
        totals[place, y - first : y - first + count] += fresh.astype(F32)

    @pl.when(edge == edges - 1)
    def _():
        half = near_top.shape[1]
        own_sum[...] = totals[:frames].astype(BF16)
        far_sum[...] = totals[frames : 2 * frames].astype(BF16)
        near_top[...] = totals[2 * frames :, :half].astype(BF16)
        near_low[...] = totals[2 * frames :, half:].astype(BF16)


def gru_of(band, meta, own, near, far_top, far_low, motion, gates, state, w_input, w_candidate, earlier):
    frames, _, height, width, chans = own.shape
    edges = state.shape[0]
    size = height // 2
    first, last = band * size, (band + 1) * size
    rows = min(last + 1, height) - max(first - 1, 0)
    sums = jax.ShapeDtypeStruct((frames, size, width, chans), BF16)
    pieces = jax.ShapeDtypeStruct((frames, size // 2, width, chans), BF16)
    sum_spec = pl.BlockSpec(sums.shape, lambda e, m: (0, 0, 0, 0))
    piece_spec = pl.BlockSpec(pieces.shape, lambda e, m: (0, 0, 0, 0))
    body = functools.partial(gru_kernel, first, last)
    operands = [meta, own, near, far_top, far_low, motion, gates, state, w_input, w_candidate]
    if earlier is None:
        kernel = lambda *refs: body(*refs[:10], None, *refs[10:])
        aliases = {}
    else:
        kernel = body
        operands.append(earlier)
        aliases = {10: 0}
    return pl.pallas_call(
        kernel,
        grid_spec=pltpu.PrefetchScalarGridSpec(
            num_scalar_prefetch=1,
            grid=(edges,),
            in_specs=[any_spec()] * 7 + [whole(w_input), whole(w_candidate)] + [any_spec()] * (len(operands) - 10),
            out_specs=[
                pl.BlockSpec((1, size, width, chans), lambda e, m: (e, band, 0, 0)),
                sum_spec,
                sum_spec,
                piece_spec,
                piece_spec,
            ],
            scratch_shapes=[
                pltpu.VMEM((2, rows, width, chans), BF16),
                pltpu.VMEM((2, rows, width, chans), BF16),
                pltpu.VMEM((2, rows, width, 2 * chans), BF16),
                pltpu.VMEM((2, rows, width, chans), BF16),
                pltpu.VMEM((rows + 2, width, 3 * chans), BF16),
                pltpu.VMEM((rows, width, chans), F32),
                pltpu.VMEM((rows, width, chans), F32),
                pltpu.VMEM((3 * frames, size, width, chans), F32),
                pltpu.SemaphoreType.DMA((5, 2)),
            ],
        ),
        out_shape=[
            jax.ShapeDtypeStruct(state.shape, BF16),
            sums,
            sums,
            pieces,
            pieces,
        ],
        input_output_aliases=aliases,
        compiler_params=pltpu.CompilerParams(vmem_limit_bytes=VMEM_LIMIT),
        cost_estimate=pl.CostEstimate(
            flops=2 * edges * rows * width * chans,
            bytes_accessed=2 * edges * rows * width * chans,
            transcendentals=0,
        ),
        name=f"gru_band{band}",
    )(*operands)


def aggregate_kernel(pieces, first, last, counts, *refs):
    sums, weights_ref, rest = refs[: 4 * len(pieces)], refs[4 * len(pieces)], refs[4 * len(pieces) + 1 :]
    out_ref, columns = rest[-2:]
    width, chans = out_ref.shape[2:]
    edge_row = jnp.zeros((1,) + columns.shape[1:], BF16)
    columns[0:1] = edge_row
    columns[columns.shape[0] - 1 :] = edge_row
    count = counts[pl.program_id(0)]
    at = 1
    for i in range(len(pieces)):
        own, far, *near = sums[4 * i : 4 * i + 4]
        top = 0
        for piece in near[pieces[i][2] :]:
            span = slice(top, top + piece.shape[1])
            total = own[0, span].astype(F32) + far[0, span].astype(F32) + piece[0].astype(F32)
            mean = (total / count).astype(BF16).astype(F32)
            put_columns(columns, at, mean)
            at += piece.shape[1]
            top += piece.shape[1]
    step = 8 if (last - first) % 5 else 5
    base = 0
    if len(rest) == 3:
        out_ref[0, :first] = rest[0][0]
        base = first
    weights = weights_ref[...]
    skip = 0 if first == 0 else 1
    for y in range(0, last - first, step):
        rows = min(step, last - first - y)
        out = conv_rows(columns, y + skip, rows, weights)
        out_ref[0, base + y : base + y + rows] = out.astype(BF16).reshape(rows, width, chans)


def aggregate_of(first, last, pieces, bands, counts, weights, earlier):
    frames, _, width, chans = bands[0][0].shape
    sums = [array for band in bands for array in band]
    depth = sum(high - low for low, high, _ in pieces)

    def blocks(band, low, high):
        specs = []
        for array in band:
            count = min(high - low, array.shape[1])
            index = low // count if array.shape[1] >= high else array.shape[1] // count - 1 if low else 0
            specs.append(pl.BlockSpec((1, count) + array.shape[2:], lambda f, c, i=index: (f, i, 0, 0)))
        return specs

    rows = last if earlier is not None else last - first
    operands = [counts, *sums, weights]
    more = []
    if earlier is not None:
        operands.append(earlier)
        more = [pl.BlockSpec((1,) + earlier.shape[1:], lambda f, c: (f, 0, 0, 0))]
    return pl.pallas_call(
        functools.partial(aggregate_kernel, pieces, first, last),
        grid_spec=pltpu.PrefetchScalarGridSpec(
            num_scalar_prefetch=1,
            grid=(frames,),
            in_specs=[spec for band, (low, high, _) in zip(bands, pieces) for spec in blocks(band, low, high)]
            + [whole(weights)]
            + more,
            out_specs=pl.BlockSpec((1, rows, width, chans), lambda f, c: (f, 0, 0, 0)),
            scratch_shapes=[pltpu.VMEM((depth + 2, width, 3 * chans), BF16)],
        ),
        out_shape=jax.ShapeDtypeStruct((frames, rows, width, chans), BF16),
        compiler_params=pltpu.CompilerParams(vmem_limit_bytes=16 << 20),
        cost_estimate=pl.CostEstimate(
            flops=2 * frames * (last - first) * width * 9 * chans * chans,
            bytes_accessed=8 * frames * depth * width * chans,
            transcendentals=0,
        ),
        name=f"aggregate_from{first}",
    )(*operands)


def per_device(
    frame_maps, net_state, edges, offsets, w_motion, w_input, w_gates, w_candidate, w_aggregate
):
    frames, _, height, width, chans = frame_maps.shape
    edge_count = net_state.shape[0]
    me = lax.axis_index("rows")
    count = lax.axis_size("rows")
    near_route = [(i, i ^ 1) for i in range(count)]
    far_route = [(i, i + 1 if i % 2 else i - 1) for i in range(1, count - 1)]

    def far_swap(block, *after):
        if after:
            block = lax.optimization_barrier((block,) + after)[0]
        return lax.ppermute(block, "rows", far_route)

    def near_swap(block):
        return lax.ppermute(block, "rows", near_route)

    features = frame_maps[:, 0]
    far_feat = far_swap(features)
    near = near_swap(lax.optimization_barrier((frame_maps, features))[0])

    my_edges = lax.dynamic_slice_in_dim(edges, me * edge_count, edge_count, 0)
    owner = my_edges // frames
    buf = jnp.where(owner == me, 0, jnp.where(owner == (me ^ 1), 2, 1))
    local = my_edges % frames
    meta = jnp.stack(
        [buf[:, 0], local[:, 0], buf[:, 1], local[:, 1], offsets[:, 0], offsets[:, 1]], axis=1
    ).astype(jnp.int32)
    mine = me * frames + jnp.arange(frames, dtype=jnp.int32)
    counts = jnp.maximum(jnp.sum((edges[:, 0][:, None] == mine[None]).astype(F32), axis=0), 1.0)

    base = motion_weights(w_motion, width)
    gates = gates_of(net_state, lax.optimization_barrier((w_gates, near))[0])
    half = 3 * edge_count // 4
    split = height // 2 + 1
    later_maps = lax.optimization_barrier((frame_maps, near))[0]
    context_top, context_low = later_maps[:, 1, :split], later_maps[:, 1, split:]
    held_meta = lax.optimization_barrier((meta, gates, context_top, context_low))[0]
    motion = motion_of(0, half, held_meta, frame_maps, near, far_feat, base, None)
    far_top = far_swap(context_top, motion)
    far_low = far_swap(context_low, motion)
    motion = motion_of(half, edge_count, meta, frame_maps, near, far_feat, base, motion)

    def gru(band, earlier):
        fars = (far_top, far_low if band else far_top)
        return gru_of(band, meta, frame_maps, near, *fars, motion, gates, net_state, w_input, w_candidate, earlier)

    new_state, own_first, far_sum, *near_first = gru(0, None)
    far_first = far_swap(far_sum)
    new_state, own_second, far_sum, *near_second = gru(1, new_state)
    far_second = far_swap(far_sum)
    near_first, near_second = (
        [near_swap(piece) for piece in lax.optimization_barrier((*pieces, far_first))[:2]]
        for pieces in (near_first, near_second)
    )
    first = (own_first, far_first, *near_first)
    second = (own_second, far_second, *near_second)
    size = height // 2
    upper = aggregate_of(0, size - 1, ((0, size, 0),), (first,), counts, w_aggregate, None)
    frame_update = aggregate_of(
        size - 1, height, ((size - 2, size, 1), (0, size, 0)), (first, second), counts, w_aggregate, upper
    )
    return (new_state, frame_update)


def solution(mesh):
    in_specs = (
        P(("groups", "rows"), None, None, None, None),
        P(("groups", "rows"), None, None, None),
        P("groups", None),
        P(("groups", "rows"), None),
        P(),
        P(),
        P(),
        P(),
        P(),
    )
    out_specs = (P(("groups", "rows"), None, None, None), P(("groups", "rows"), None, None, None))
    return jax.shard_map(
        per_device, mesh=mesh, in_specs=in_specs, out_specs=out_specs, check_vma=False
    )
```
